256 devices in a mesh: node: 32 (over z, y), mp: 8 (over x, core).
Axes of the slice: x: 4, y: 4, z: 8, core: 2. Of those that a mesh axis runs over, the one named last changes fastest.
Arguments:
- queries: bfloat16 [4, 4096, 5120], P(None, 'node', 'mp'), may hold values from -200 to 200
- keys: bfloat16 [4, 4096, 1024], P(None, ('node', 'mp')), may hold values from -8 to 8
- values: bfloat16 [4, 4096, 1024], P(None, ('node', 'mp')), may hold values from -6 to 6
- grad_out: bfloat16 [4, 4096, 5120], P(None, 'node', 'mp'), may hold values from -6 to 6
- lengths: int32 [4, 32], P(None, 'node'), may hold values from 1 to 128, as said below
- parents: int32 [3, 32], P(None, 'node'), may hold values from 0 to 31, as said below
Outputs:
- attended: bfloat16 [4, 4096, 5120], P(None, 'node', 'mp')
- grad_queries: bfloat16 [4, 4096, 5120], P(None, 'node', 'mp')
- grad_keys: bfloat16 [4, 4096, 1024], P(None, ('node', 'mp'))
- grad_values: bfloat16 [4, 4096, 1024], P(None, ('node', 'mp'))
The draws below stay inside these ranges and needn't reach their ends.
Inputs may be any that keep to these rules, and one draw needn't show every extreme that they name: `lengths`: each node's valid tokens are its leading positions; some node of every level has 128 of them and some node has one. parents[a, j] is the slot at level a of the parent of node j at level a + 1; its remainder on division by 4 - 1 is a.
All inputs are finite; a program needn't handle non-finite values.
Results may differ from the reference program's by a relative error of at most 0.015.
Values may be sent and summed in bfloat16 or wider, within the bound.
A program may use at most 64 MiB of HBM per device.

```python
import math
import jax
import jax.numpy as jnp
from jax import lax

QH = 40
KVH = 8
HD = 128
SEG = 128
LEVELS = 4
NODES = 32
ROWS = 4096


def shared_keys(key):
    base = jax.random.normal(key, (LEVELS, NODES * SEG, KVH * HD), jnp.float32)
    return base


def draw_keys(key, part):
    base = shared_keys(key)
    return base.astype(jnp.bfloat16)


def draw_queries(key, part):
    key = jax.random.fold_in(key, 7)
    drawn = jax.random.normal(key, (LEVELS, NODES * SEG, QH * HD), jnp.float32)
    return drawn.astype(jnp.bfloat16)


def draw_lengths(key, part):
    key = jax.random.fold_in(key, 5)
    first, second, third, fourth = jax.random.split(key, 4)
    raw = jax.random.randint(first, (LEVELS, NODES), SEG // 4, SEG + 1)
    halving = jax.random.randint(second, (LEVELS, NODES), 0, 2)
    shrunk = jnp.maximum(raw // jnp.left_shift(1, halving), 1)
    full_slot = jax.random.randint(third, (LEVELS, 1), 0, NODES)
    one_slot = (full_slot + 1 + jax.random.randint(fourth, (LEVELS, 1), 0, NODES - 1)) % NODES
    slot_ids = jnp.arange(NODES)[None, :]
    shaped = jnp.where(slot_ids == full_slot, SEG, shrunk)
    shaped = jnp.where(slot_ids == one_slot, 1, shaped)
    return shaped.astype(jnp.int32)


def draw_parents(key, part):
    key = jax.random.fold_in(key, 9)
    first, second, third = jax.random.split(key, 3)
    stride = LEVELS - 1
    level_ids = jnp.arange(LEVELS - 1, dtype=jnp.int32)[:, None]
    counts = (NODES - 1 - level_ids) // stride + 1
    picks = jax.random.randint(first, (LEVELS - 1, NODES), 0, counts)
    raw = level_ids + stride * picks
    top_level = (NODES - 1) % stride
    high_slot = jax.random.randint(second, (), 0, NODES)
    low_slot = (high_slot + 1 + jax.random.randint(third, (), 0, NODES - 1)) % NODES
    slot_ids = jnp.arange(NODES)[None, :]
    raw = jnp.where((level_ids == top_level) & (slot_ids == high_slot), NODES - 1, raw)
    raw = jnp.where((level_ids == 0) & (slot_ids == low_slot), 0, raw)
    return raw.astype(jnp.int32)


def levels(own_key, extent, pieces, smallest, high):
    level, own = 1.0, jax.random.fold_in(own_key, 6)
    for position, blocks in pieces:
        draws = jnp.exp(jax.random.uniform(jax.random.fold_in(own, position), (blocks,), jnp.float32, smallest / len(pieces), high / len(pieces)))
        level = level * jnp.repeat(draws, extent[position] // blocks).reshape([-1 if axis == position else 1 for axis in range(len(extent))])
    return level


def normal_values(own_key, extent, scale, most, cuts=(), kind=jnp.bfloat16):
    entries = jax.random.normal(own_key, extent, jnp.float32) * scale
    if len(cuts) > 0:
        entries = levels(own_key, extent, cuts, -0.22, 0.18) * entries
    return jnp.clip(entries, min=-most, max=most).astype(kind)


def setup_inputs(seed: int = 0) -> dict:
    seeds = jax.random.split(jax.random.key(seed), 7)
    return {
        "queries": draw_queries(jax.random.fold_in(seeds[6], 71), 0),
        "keys": draw_keys(jax.random.fold_in(seeds[6], 71), 0),
        "values": normal_values(seeds[2], (LEVELS, ROWS, KVH * HD), 1.0, 6.0, ((1, 256),)),
        "grad_out": normal_values(seeds[3], (LEVELS, ROWS, QH * HD), 1.0, 6.0, ((1, 32), (2, 8))),
        "lengths": draw_lengths(jax.random.fold_in(seeds[6], 71), 0),
        "parents": draw_parents(jax.random.fold_in(seeds[6], 71), 0),
    }


def product(form, left, right):
    return jnp.einsum(form, left.astype(jnp.float32), right.astype(jnp.float32))

def attend(query, key_cat, value_cat, cotangent, limits):
    seg_len = query.shape[0]
    context = key_cat.shape[0]
    kv_heads = key_cat.shape[1] // HD
    groups = query.shape[1] // (kv_heads * HD)
    scale = 1.0 / math.sqrt(HD)
    query_heads = query.reshape(seg_len, kv_heads, groups, HD)
    key_heads = key_cat.reshape(context, kv_heads, HD)
    value_heads = value_cat.reshape(context, kv_heads, HD)
    scores = product('sngd,tnd->ngst', query_heads, key_heads) * scale
    col_ids = jnp.arange(context)
    row_ids = jnp.arange(seg_len)
    place = col_ids % seg_len
    limit = jnp.repeat(limits, seg_len, total_repeat_length=context)
    own_start = context - seg_len
    allowed = (place[None, :] < limit[None, :]) & ((col_ids[None, :] < own_start) | (place[None, :] <= row_ids[:, None]))
    live = row_ids < limits[-1]
    scores = jnp.where(allowed, scores, -jnp.inf)
    row_max = lax.optimization_barrier(jnp.max(scores, axis=-1, keepdims=True))
    weights = jnp.exp(scores - row_max)
    probs = weights / lax.optimization_barrier(jnp.sum(weights, axis=-1, keepdims=True))
    probs_low = probs.astype(jnp.bfloat16)
    mixed = product('ngst,tnd->sngd', probs_low, value_heads)
    mixed = jnp.where(live[:, None, None, None], mixed, 0.0)
    attended = mixed.reshape(seg_len, -1).astype(jnp.bfloat16)
    grad_ctx = jnp.where(live[:, None], cotangent, jnp.zeros_like(cotangent)).reshape(seg_len, kv_heads, groups, HD)
    grad_probs = product('sngd,tnd->ngst', grad_ctx, value_heads)
    inner = lax.optimization_barrier(jnp.sum(probs * grad_probs, axis=-1, keepdims=True))
    grad_scores = (probs * (grad_probs - inner) * scale).astype(jnp.bfloat16)
    grad_query = product('ngst,tnd->sngd', grad_scores, key_heads).reshape(seg_len, -1).astype(jnp.bfloat16)
    grad_key = product('ngst,sngd->tnd', grad_scores, query_heads).reshape(context, -1)
    grad_value = product('ngst,sngd->tnd', probs_low, grad_ctx).reshape(context, -1)
    return (attended, grad_query, grad_key, grad_value)

def reference(queries, keys, values, grad_out, lengths, parents):
    width = KVH * HD
    query_blocks = queries.reshape(LEVELS, NODES, SEG, QH * HD)
    grad_blocks = grad_out.reshape(LEVELS, NODES, SEG, QH * HD)
    key_blocks = keys.reshape(LEVELS, NODES, SEG, width)
    value_blocks = values.reshape(LEVELS, NODES, SEG, width)
    node_ids = jnp.arange(NODES, dtype=jnp.int32)
    chains = []
    for level in range(LEVELS):
        links = [None] * level
        current = node_ids
        for upper in reversed(range(level)):
            current = parents[upper][current].astype(jnp.int32)
            links[upper] = current
        chains.append(links)
    attended_all = []
    grad_query_all = []
    own_terms = []
    block_terms = []
    for level in range(LEVELS):
        key_cat = jnp.concatenate([key_blocks[upper][chains[level][upper]] for upper in range(level)] + [key_blocks[level]], axis=1)
        value_cat = jnp.concatenate([value_blocks[upper][chains[level][upper]] for upper in range(level)] + [value_blocks[level]], axis=1)
        limits = jnp.stack([lengths[upper][chains[level][upper]] for upper in range(level)] + [lengths[level]], axis=1)
        results = lax.map(lambda items: attend(*items), (query_blocks[level], key_cat, value_cat, grad_blocks[level], limits))
        attended_all.append(results[0])
        grad_query_all.append(results[1])
        both = jnp.concatenate((results[2], results[3]), axis=2)
        own_terms.append(both[:, level * SEG:])
        block_terms.append([both[:, upper * SEG:(upper + 1) * SEG] for upper in range(level)])
    grad_key_all = []
    grad_value_all = []
    for upper in range(LEVELS):
        total = own_terms[upper]
        if upper < LEVELS - 1:
            stacked = jnp.stack([block_terms[level][upper] for level in range(upper + 1, LEVELS)])
            owners = jnp.stack([chains[level][upper] for level in range(upper + 1, LEVELS)])

            def arrive(target, stacked=stacked, owners=owners):
                partial_sum = lax.optimization_barrier(jnp.sum(jnp.where((owners == target)[:, :, None, None], stacked, 0.0), axis=0))
                rounded = lax.optimization_barrier(partial_sum.astype(jnp.bfloat16))
                return lax.optimization_barrier(jnp.sum(rounded.astype(jnp.float32), axis=0))
            total = total + lax.map(arrive, node_ids)
        grad_key_all.append(total[..., :width].astype(jnp.bfloat16))
        grad_value_all.append(total[..., width:].astype(jnp.bfloat16))
    return (jnp.stack(attended_all).reshape(LEVELS, ROWS, QH * HD), jnp.stack(grad_query_all).reshape(LEVELS, ROWS, QH * HD), jnp.stack(grad_key_all).reshape(LEVELS, ROWS, width), jnp.stack(grad_value_all).reshape(LEVELS, ROWS, width))
```

```python
import functools
import math

import jax
import jax.numpy as jnp
from jax import lax
from jax.experimental import pallas as pl
from jax.experimental.pallas import tpu as pltpu
from jax.sharding import PartitionSpec as P

HD = 128
SEG = 128
NZ, NY = 8, 4
NODES = NZ * NY
MP = 8
LEVELS = 4
GROUPS = 5
QR = GROUPS * SEG
TOK = SEG // MP
HALF = SEG // 2
F32 = jnp.float32
BF16 = jnp.bfloat16
MESH = pl.DeviceIdType.MESH
SCALE = 1.0 / math.sqrt(HD)
EXP2_SCALE = SCALE * math.log2(math.e)
CH = 32
REACH = [(4, 3), (3, 4), (4, 3), (3, 4), (4, 3)]


def dot(a, b, ca, cb):
    return lax.dot_general(a, b, (((ca,), (cb,)), ((), ())), preferred_element_type=F32)


def attend(level, limits, kv_blocks, kc, vc, qs, dos, st, dp, plow, dsl, att_v, gq_v, term):
    ctx = (level + 1) * SEG
    for b, block in enumerate(kv_blocks):
        kc[b * SEG:(b + 1) * SEG, :] = block[:, :HD]
        vc[b * SEG:(b + 1) * SEG, :] = block[:, HD:]
    own_len = limits[-1]
    live_rows = lax.broadcasted_iota(jnp.int32, (SEG, HD), 0) < own_len
    for g in range(GROUPS):
        rows = slice(g * SEG, (g + 1) * SEG)
        dos[level, rows, :] = jnp.where(live_rows, dos[level, rows, :], jnp.zeros((), BF16))
    q = qs[level]
    d = dos[level]
    st[:ctx, :] = dot(kc[:ctx, :], q, 1, 1)
    dp[:ctx, :] = dot(vc[:ctx, :], d, 1, 1)
    peak = jnp.full((8, QR), -jnp.inf, F32)
    for r in range(0, ctx, CH):
        b, off = r // SEG, r % SEG
        place = lax.broadcasted_iota(jnp.int32, (CH, QR), 0) + off
        ok = place < limits[b]
        if b == level:
            ok = ok & (place <= (lax.broadcasted_iota(jnp.int32, (CH, QR), 1) & (SEG - 1)))
        s = jnp.where(ok, st[r:r + CH, :], -jnp.inf)
        st[r:r + CH, :] = s
        for i in range(0, CH, 8):
            peak = jnp.maximum(peak, s[i:i + 8, :])
    peak = jnp.max(peak, axis=0, keepdims=True)
    total = jnp.zeros((8, QR), F32)
    for r in range(0, ctx, CH):
        e = jnp.exp2((st[r:r + CH, :] - peak) * EXP2_SCALE)
        st[r:r + CH, :] = e
        for i in range(0, CH, 8):
            total = total + e[i:i + 8, :]
    inv = 1.0 / jnp.sum(total, axis=0, keepdims=True)
    inner = jnp.zeros((8, QR), F32)
    for r in range(0, ctx, CH):
        p = st[r:r + CH, :] * inv
        st[r:r + CH, :] = p
        plow[r:r + CH, :] = p.astype(BF16)
        prod = p * dp[r:r + CH, :]
        for i in range(0, CH, 8):
            inner = inner + prod[i:i + 8, :]
    inner = jnp.sum(inner, axis=0, keepdims=True)
    for r in range(0, ctx, CH):
        dsl[r:r + CH, :] = (st[r:r + CH, :] * (dp[r:r + CH, :] - inner)).astype(BF16)
    term[level, :ctx, HD:] = dot(plow[:ctx, :], d, 1, 0)
    term[level, :ctx, :HD] = dot(dsl[:ctx, :], q, 1, 0) * SCALE
    out_t = dot(vc[:ctx, :], plow[:ctx, :], 0, 0)
    gq_t = dot(kc[:ctx, :], dsl[:ctx, :], 0, 0) * SCALE
    for g in range(GROUPS):
        rows = slice(g * SEG, (g + 1) * SEG)
        o = jnp.transpose(out_t[:, rows])
        att_v[level, rows, :] = jnp.where(live_rows, o, 0.0).astype(BF16)
        gq_v[level, rows, :] = jnp.transpose(gq_t[:, rows]).astype(BF16)


def kernel(q_hbm, k_hbm, v_hbm, do_hbm, len_s, par_s,
           att_hbm, gq_hbm, gk_hbm, gv_hbm,
           qs, dos, kvl, kvg, meta, meta_s, anc_s,
           kc, vc, st, dp, plow, dsl, att_v, gq_v, term, cbuf, gfin,
           rz, rz0, ry_a, sy_a, ry_b, sy_b,
           loc_sem, meta_ss, meta_rs, a2a_ss, a2a_rs, agz_ss, agz_rs, agy_ss, agy_rs,
           rsz_ss, rsz_rs, rsy_ss, rsy_rs, back_ss, back_rs):
    n = lax.axis_index("node")
    m = lax.axis_index("mp")
    z = n // NY
    y = lax.rem(n, NY)
    own_class = lax.rem(n, LEVELS - 1)

    def node(dz, dy):
        return lax.rem(z + (dz + NZ), NZ) * NY + lax.rem(y + (dy + NY), NY)

    def peer(d):
        return lax.rem(m + (d + MP), MP)

    def to_node(src, dst, ss, rs, target):
        return pltpu.make_async_remote_copy(src_ref=src, dst_ref=dst, send_sem=ss, recv_sem=rs,
                                            device_id={"node": target}, device_id_type=MESH)

    def to_mp(src, dst, ss, rs, target):
        return pltpu.make_async_remote_copy(src_ref=src, dst_ref=dst, send_sem=ss, recv_sem=rs,
                                            device_id={"mp": target}, device_id_type=MESH)

    sends = []

    def launch(copy):
        copy.start()
        sends.append(copy)

    local = []
    for g in range(GROUPS):
        lanes = pl.ds(g * HD, HD)
        for i, (src, dst) in enumerate(((q_hbm, qs), (do_hbm, dos))):
            c = pltpu.make_async_copy(src.at[:, :, lanes], dst.at[:, pl.ds(g * SEG, SEG), :], loc_sem.at[2 * g + i])
            c.start()
            local.append(c)
    own_tok = pl.ds(m * TOK, TOK)
    own_lanes = pl.ds(m * HD, HD)
    mine = []
    for i, src in enumerate((k_hbm, v_hbm)):
        half = pl.ds(i * HD, HD)
        c = pltpu.make_async_copy(src.at[own_class, :, own_lanes], kvg.at[n, own_tok, half], loc_sem.at[10 + i])
        c.start()
        mine.append(c)
        c = pltpu.make_async_copy(src.at[:, :, own_lanes], kvl.at[:, own_tok, half], loc_sem.at[12 + i])
        c.start()
        local.append(c)

    barrier = pltpu.get_barrier_semaphore()
    for d in range(1, MP):
        pl.semaphore_signal(barrier, inc=1, device_id={"mp": peer(d)}, device_id_type=MESH)
    for d in range(1, NY):
        pl.semaphore_signal(barrier, inc=1, device_id={"node": node(0, d)}, device_id_type=MESH)
    for d in range(1, NZ):
        pl.semaphore_signal(barrier, inc=1, device_id={"node": node(d, 0)}, device_id_type=MESH)
    lane = lax.broadcasted_iota(jnp.int32, (1, 128), 1)
    row = jnp.zeros((1, 128), jnp.int32)
    for level in range(LEVELS):
        row = jnp.where(lane == level, len_s[level, 0], row)
    for level in range(LEVELS - 1):
        row = jnp.where(lane == LEVELS + level, par_s[level, 0], row)
    meta[n] = row
    pl.semaphore_wait(barrier, (MP - 1) + (NY - 1) + (NZ - 1))

    for d in range(1, MP):
        p = peer(d)
        for i, src in enumerate((k_hbm, v_hbm)):
            launch(to_mp(src.at[own_class, :, pl.ds(p * HD, HD)], kvg.at[n, own_tok, pl.ds(i * HD, HD)],
                         a2a_ss.at[0, d, i], a2a_rs.at[0, d, i], p))
    for d in range(1, NY):
        launch(to_node(meta.at[n], meta.at[n], meta_ss.at[0, d], meta_rs.at[0, d], node(0, d)))
    for d in range(1, MP):
        p = peer(d)
        for i, src in enumerate((k_hbm, v_hbm)):
            launch(to_mp(src.at[:, :, pl.ds(p * HD, HD)], kvl.at[:, own_tok, pl.ds(i * HD, HD)],
                         a2a_ss.at[1, d, i], a2a_rs.at[1, d, i], p))

    def a2a_wait(which, d):
        tok = pl.ds(peer(-d) * TOK, TOK)
        for i, src in enumerate((k_hbm, v_hbm)):
            half = pl.ds(i * HD, HD)
            if which == 0:
                c = to_mp(src.at[own_class, :, own_lanes], kvg.at[n, tok, half], a2a_ss.at[0, d, i], a2a_rs.at[0, d, i], peer(-d))
            else:
                c = to_mp(src.at[:, :, own_lanes], kvl.at[:, tok, half], a2a_ss.at[1, d, i], a2a_rs.at[1, d, i], peer(-d))
            c.wait_recv()

    for c in mine:
        c.wait()
    for d in range(1, MP):
        a2a_wait(0, d)

    def piece(slot, col):
        return kvg.at[slot, pl.ds(HALF if col == 4 else 0, HALF)]

    def ag_z(col, direction, s):
        sign = 1 if direction == 0 else -1
        dy = 0 if col == 4 else col
        src = piece(node(-sign * (s - 1), dy), col)
        return to_node(src, src, agz_ss.at[col, direction, s], agz_rs.at[col, direction, s], node(sign, 0))

    def ag_z_wait(col, direction, s):
        sign = 1 if direction == 0 else -1
        dy = 0 if col == 4 else col
        dst = piece(node(-sign * s, dy), col)
        to_node(dst, dst, agz_ss.at[col, direction, s], agz_rs.at[col, direction, s], node(-sign, 0)).wait_recv()

    def ag_y(col, t, d):
        src = piece(node(t, 0), col)
        i = 0 if col == 0 else t + 1
        return to_node(src, src, agy_ss.at[i, d], agy_rs.at[i, d], node(0, d))

    def ag_y_wait(col, t, d):
        dst = piece(node(t, -d), col)
        i = 0 if col == 0 else t + 1
        to_node(dst, dst, agy_ss.at[i, d], agy_rs.at[i, d], node(0, -d)).wait_recv()

    for d in (2, 1, 3):
        launch(ag_y(0, 0, d))
    for direction in range(2):
        launch(ag_z(4, direction, 1))
    for direction in range(2):
        launch(ag_z(0, direction, 1))
    for d in (2, 1, 3):
        launch(ag_y(4, 0, d))
    for d in range(1, NY):
        to_node(meta.at[n], meta.at[node(0, -d)], meta_ss.at[0, d], meta_rs.at[0, d], node(0, -d)).wait_recv()
    my_row = pl.ds(z * NY, NY)
    for d in range(1, NZ):
        launch(to_node(meta.at[my_row], meta.at[my_row], meta_ss.at[1, d], meta_rs.at[1, d], node(d, 0)))
    for d in (1, 3, 2):
        ag_y_wait(0, 0, d)
        for direction in range(2):
            launch(ag_z(NY - d, direction, 1))

    def gather_round(s):
        for col in (4, 0, 3, 1, 2):
            for direction in range(2):
                reach = REACH[col][direction]
                if s > reach:
                    continue
                ag_z_wait(col, direction, s)
                if s < reach:
                    launch(ag_z(col, direction, s + 1))
                if col == 4:
                    t = -s if direction == 0 else s
                    for d in (2, 1, 3):
                        launch(ag_y(4, t % NZ, d))

    gather_round(1)
    for d in range(1, NZ):
        rows = pl.ds(lax.rem(z + (NZ - d), NZ) * NY, NY)
        to_node(meta.at[my_row], meta.at[rows], meta_ss.at[1, d], meta_rs.at[1, d], node(-d, 0)).wait_recv()
    c = pltpu.make_async_copy(meta, meta_s, loc_sem.at[14])
    c.start()
    c.wait()
    gather_round(2)

    def parent(a, slot):
        return meta_s[slot, 0, LEVELS + a]

    def length(level, slot):
        return meta_s[slot, 0, level]

    chains = []
    for level in range(LEVELS):
        links = [None] * level
        slot = n
        for a in reversed(range(level)):
            slot = parent(a, slot)
            links[a] = slot
        chains.append(links)
    for a in range(LEVELS - 1):
        for level in range(1, LEVELS):
            anc_s[a * 3 + level - 1] = chains[level][a] if level > a else jnp.int32(-1)
    gather_round(3)
    for c in local:
        c.wait()
    for d in range(1, MP):
        a2a_wait(1, d)

    def run_level(level):
        limits = [length(a, chains[level][a]) for a in range(level)] + [length(level, n)]
        blocks = [kvg[chains[level][a]] for a in range(level)] + [kvl[level]]
        attend(level, limits, blocks, kc, vc, qs, dos, st, dp, plow, dsl, att_v, gq_v, term)
        for g in range(GROUPS):
            lanes = pl.ds(g * HD, HD)
            for i, (src, dst) in enumerate(((att_v, att_hbm), (gq_v, gq_hbm))):
                launch_local(pltpu.make_async_copy(src.at[level, pl.ds(g * SEG, SEG), :], dst.at[level, :, lanes],
                                                   loc_sem.at[16 + (level * GROUPS + g) * 2 + i]))

    stores = []

    def launch_local(copy):
        copy.start()
        stores.append(copy)

    run_level(0)
    gather_round(4)
    for t in (0, 1, 7, 2, 6, 3, 5, 4):
        for d in (1, 3, 2):
            ag_y_wait(4, t, d)
    for level in (3, 2, 1):
        run_level(level)

    for a in range(LEVELS - 1):
        names = list(range(a + 1, LEVELS))
        for bits in range(1 << len(names)):
            slot = a * 8 + (bits << a)
            for r in range(0, SEG, CH):
                acc = None
                for i, level in enumerate(names):
                    if bits >> i & 1:
                        x = term[level, a * SEG + r:a * SEG + r + CH, :]
                        acc = x if acc is None else acc + x
                if acc is None:
                    acc = jnp.zeros((CH, 2 * HD), F32)
                cbuf[slot, r:r + CH, :] = acc.astype(BF16)

    def own_part(target, col):
        a = lax.rem(target, 3)
        hit = [(anc_s[a * 3 + i] == target).astype(jnp.int32) for i in range(3)]
        slot = a * 8 + hit[0] + 2 * hit[1] + 4 * hit[2]
        return cbuf[slot, pl.ds(HALF if col == 4 else 0, HALF), :].astype(F32)

    def rs_y_b(t, d):
        return to_node(sy_b.at[t, d], ry_b.at[t, d], rsy_ss.at[t, d], rsy_rs.at[t, d], node(0, d))

    def rs_y_a(d):
        return to_node(sy_a.at[d], ry_a.at[d], rsy_ss.at[NZ, d], rsy_rs.at[NZ, d], node(0, d))

    def rs_z(col, direction, t, first):
        sign = 1 if direction == 0 else -1
        src = rz0.at[col, direction] if first else rz.at[col, direction, t]
        return to_node(src, rz.at[col, direction, t - 1], rsz_ss.at[col, direction, t], rsz_rs.at[col, direction, t - 1],
                       node(sign, 0))

    def rs_z_wait(col, direction, t):
        sign = 1 if direction == 0 else -1
        dst = rz.at[col, direction, t]
        to_node(dst, dst, rsz_ss.at[col, direction, t], rsz_rs.at[col, direction, t], node(-sign, 0)).wait_recv()

    def total_b(t):
        acc = own_part(node(t, 0), 4)
        for d in range(1, NY):
            to_node(sy_b.at[t, d], ry_b.at[t, d], rsy_ss.at[t, d], rsy_rs.at[t, d], node(0, -d)).wait_recv()
            acc = acc + ry_b[t, d].astype(F32)
        return acc

    for t in (4, 5, 3, 6, 2, 7, 1, 0):
        for d in (2, 1, 3):
            sy_b[t, d] = own_part(node(t, d), 4).astype(BF16)
            launch(rs_y_b(t, d))
    for col in (2, 1, 3, 0):
        for direction in range(2):
            t = REACH[col][direction]
            rz0[col, direction] = own_part(node(t if direction == 0 else -t, col), col).astype(BF16)
            launch(rs_z(col, direction, t, True))
    for i in range(1, LEVELS):
        level = lax.rem(own_class + i, LEVELS)
        gfin[level] = term[level, pl.ds(level * SEG, SEG), :].astype(BF16)

    def send_back(level, d, which):
        p = peer(d)
        for i, dst in enumerate((gk_hbm, gv_hbm)):
            launch(to_mp(gfin.at[level, pl.ds(p * TOK, TOK), pl.ds(i * HD, HD)], dst.at[level, :, own_lanes],
                         back_ss.at[which, d, i], back_rs.at[which, d, i], p))

    def keep(level, which):
        for i, dst in enumerate((gk_hbm, gv_hbm)):
            launch_local(pltpu.make_async_copy(gfin.at[level, own_tok, pl.ds(i * HD, HD)], dst.at[level, :, own_lanes],
                                               loc_sem.at[56 + which * 2 + i]))

    for i in range(1, LEVELS):
        level = lax.rem(own_class + i, LEVELS)
        keep(level, i)
        for d in range(1, MP):
            send_back(level, d, i)

    for step in range(0, 5):
        for col in (4, 2, 1, 3, 0):
            for direction in range(2):
                reach = REACH[col][direction]
                t = reach - step
                if t < 0 or (step == 0 and col != 4):
                    continue
                if step > 0:
                    rs_z_wait(col, direction, t)
                if t == 0:
                    continue
                rel = t if direction == 0 else -t
                acc = total_b(rel % NZ) if col == 4 else own_part(node(rel, col), col)
                if step == 0:
                    rz0[col, direction] = acc.astype(BF16)
                else:
                    rz[col, direction, t] = (acc + rz[col, direction, t].astype(F32)).astype(BF16)
                launch(rs_z(col, direction, t, step == 0))
    for col in (2, 1, 3):
        acc = own_part(node(0, col), col) + rz[col, 0, 0].astype(F32) + rz[col, 1, 0].astype(F32)
        sy_a[col] = acc.astype(BF16)
        launch(rs_y_a(col))
    own_row = own_class * SEG
    low = total_b(0) + rz[4, 0, 0].astype(F32) + rz[4, 1, 0].astype(F32)
    gfin[own_class, pl.ds(HALF, HALF), :] = (low + term[own_class, pl.ds(own_row + HALF, HALF), :]).astype(BF16)
    high = own_part(n, 0) + rz[0, 0, 0].astype(F32) + rz[0, 1, 0].astype(F32)
    for d in range(1, NY):
        to_node(sy_a.at[d], ry_a.at[d], rsy_ss.at[NZ, d], rsy_rs.at[NZ, d], node(0, -d)).wait_recv()
        high = high + ry_a[d].astype(F32)
    gfin[own_class, pl.ds(0, HALF), :] = (high + term[own_class, pl.ds(own_row, HALF), :]).astype(BF16)
    keep(own_class, 0)
    for d in range(1, MP):
        send_back(own_class, d, 0)

    for which in range(LEVELS):
        level = lax.rem(own_class + which, LEVELS)
        for d in range(1, MP):
            p = peer(-d)
            for i, dst in enumerate((gk_hbm, gv_hbm)):
                to_mp(gfin.at[level, pl.ds(p * TOK, TOK), pl.ds(i * HD, HD)], dst.at[level, :, pl.ds(p * HD, HD)],
                      back_ss.at[which, d, i], back_rs.at[which, d, i], p).wait_recv()
    for c in stores:
        c.wait()
    for c in sends:
        c.wait_send()


def per_device(queries, keys, values, grad_out, lengths, parents):
    hbm = pl.BlockSpec(memory_space=pl.ANY)
    smem = pl.BlockSpec(memory_space=pltpu.SMEM)
    dma = pltpu.SemaphoreType.DMA
    vm = pltpu.VMEM
    ctx = LEVELS * SEG
    return tuple(pl.pallas_call(
        kernel,
        out_shape=(
            jax.ShapeDtypeStruct(queries.shape, BF16),
            jax.ShapeDtypeStruct(queries.shape, BF16),
            jax.ShapeDtypeStruct(keys.shape, BF16),
            jax.ShapeDtypeStruct(keys.shape, BF16),
        ),
        in_specs=[hbm, hbm, hbm, hbm, smem, smem],
        out_specs=(hbm, hbm, hbm, hbm),
        scratch_shapes=[
            vm((LEVELS, QR, HD), BF16), vm((LEVELS, QR, HD), BF16),
            vm((LEVELS, SEG, 2 * HD), BF16), vm((NODES, SEG, 2 * HD), BF16),
            vm((NODES, 1, 128), jnp.int32), pltpu.SMEM((NODES, 1, 128), jnp.int32), pltpu.SMEM((9,), jnp.int32),
            vm((ctx, HD), BF16), vm((ctx, HD), BF16),
            vm((ctx, QR), F32), vm((ctx, QR), F32), vm((ctx, QR), BF16), vm((ctx, QR), BF16),
            vm((LEVELS, QR, HD), BF16), vm((LEVELS, QR, HD), BF16),
            vm((LEVELS, ctx, 2 * HD), F32), vm((24, SEG, 2 * HD), BF16), vm((LEVELS, SEG, 2 * HD), BF16),
            vm((5, 2, 4, HALF, 2 * HD), BF16), vm((5, 2, HALF, 2 * HD), BF16),
            vm((NY, HALF, 2 * HD), BF16), vm((NY, HALF, 2 * HD), BF16),
            vm((NZ, NY, HALF, 2 * HD), BF16), vm((NZ, NY, HALF, 2 * HD), BF16),
            dma((64,)), dma((2, NZ)), dma((2, NZ)), dma((2, MP, 2)), dma((2, MP, 2)),
            dma((5, 2, 5)), dma((5, 2, 5)), dma((NZ + 1, NY)), dma((NZ + 1, NY)),
            dma((5, 2, 5)), dma((5, 2, 5)), dma((NZ + 1, NY)), dma((NZ + 1, NY)),
            dma((LEVELS, MP, 2)), dma((LEVELS, MP, 2)),
        ],
        compiler_params=pltpu.CompilerParams(collective_id=0, has_side_effects=True, vmem_limit_bytes=48 << 20),
        name="tree_attention",
    )(queries, keys, values, grad_out, lengths, parents))


def solution(mesh):
    placed = (
        P(None, "node", "mp"),
        P(None, ("node", "mp"), None),
        P(None, ("node", "mp"), None),
        P(None, "node", "mp"),
        P(None, "node"),
        P(None, "node"),
    )
    return jax.shard_map(
        per_device,
        mesh=mesh,
        in_specs=placed,
        out_specs=(
            P(None, "node", "mp"),
            P(None, "node", "mp"),
            P(None, ("node", "mp"), None),
            P(None, ("node", "mp"), None),
        ),
        check_vma=False,
    )
```

```python
import math

import jax
import jax.numpy as jnp
from jax import lax
from jax.experimental import pallas as pl
from jax.experimental.pallas import tpu as pltpu
from jax.sharding import PartitionSpec as P

HD = 128
SEG = 128
NZ, NY = 8, 4
NODES = NZ * NY
MP = 8
LEVELS = 4
GROUPS = 5
QR = GROUPS * SEG
TOK = SEG // MP
CTX_ROWS = SEG * LEVELS * (LEVELS + 1) // 2
SETS = 24
F32 = jnp.float32
BF16 = jnp.bfloat16
MESH = pl.DeviceIdType.MESH
SCALE = 1.0 / math.sqrt(HD)
EXP2_SCALE = SCALE * math.log2(math.e)
CH = 32
KEY, VALUE = 0, 1
HOP, META, SHARE, GATHER, SCATTER, LAST, BACK = range(7)
REACH = [(4, 3), (3, 4), (4, 3), (3, 4), (4, 3)]
COLS = (2, 1, 3, 0)
NEAR = [(0, 0), (0, 1), (0, 2), (0, 3), (1, 0), (-1, 0)]
HOPS = [(KEY, 2), (VALUE, 4), (VALUE, 5), (KEY, 1), (KEY, 3), (KEY, 0), (VALUE, 0)]


def dot(a, b, ca, cb):
    return lax.dot_general(a, b, (((ca,), (cb,)), ((), ())), preferred_element_type=F32)


def context(level):
    first = SEG * level * (level + 1) // 2
    return first, (level + 1) * SEG


def kernel(q_hbm, k_hbm, v_hbm, do_hbm, len_s, par_s,
           att_hbm, gq_hbm, gk_o, gv_o,
           ksrc, vsrc, qs, dos, kvl, kg, vg, meta, meta_s, set_s,
           kc, vc, st, dp, plow, dsl, att_v, gq_v, term, cbuf, gfin,
           rz, rz0, ry, sy, last, got, rows_out,
           sent, loc_sem, send_sem, meta_rs, a2a_rs, hop_rs, agz_rs, agy_rs, rsz_rs, rsy_rs, end_rs, back_rs):
    n = lax.axis_index("node")
    m = lax.axis_index("mp")
    z = n >> 2
    y = n & (NY - 1)
    own_class = lax.rem(n, LEVELS - 1)
    sources = (ksrc, vsrc)
    results = (gk_o, gv_o)
    gathered = (kg, vg)

    def node(dz, dy):
        up = ((z + dz) & (NZ - 1)) << 2 if dz % NZ else z << 2
        return up | ((y + dy) & (NY - 1) if dy % NY else y)

    def peer(d):
        return (m + d) & (MP - 1)

    def remote(src, dst, ss, rs, to):
        pltpu.make_async_remote_copy(src_ref=src, dst_ref=dst, send_sem=send_sem.at[ss], recv_sem=rs,
                                     device_id=to, device_id_type=MESH).start()

    def to_node(src, dst, ss, rs, target):
        remote(src, dst, ss, rs, {"node": target})

    def to_mp(src, dst, ss, rs, target):
        remote(src, dst, ss, rs, {"mp": target})

    def to_any(src, dst, ss, rs, target, p):
        remote(src, dst, ss, rs, {"node": target, "mp": p})

    def arrived(ref, sem):
        pltpu.make_async_copy(ref, ref, sem).wait()

    def local(src, dst, sem):
        pltpu.make_async_copy(src, dst, sem).start()

    own_tok = pl.ds(m * TOK, TOK)
    own_lanes = pl.ds(m * HD, HD)
    for kv, src in enumerate((k_hbm, v_hbm)):
        local(src, sources[kv], loc_sem.at[kv])
    for g in range(GROUPS):
        lanes = pl.ds(g * HD, HD)
        for i, (src, dst) in enumerate(((q_hbm, qs), (do_hbm, dos))):
            local(src.at[:, :, lanes], dst.at[:, pl.ds(g * SEG, SEG), :], loc_sem.at[2 + i])

    barrier = pltpu.get_barrier_semaphore()
    for d in range(1, MP):
        pl.semaphore_signal(barrier, inc=1, device_id={"mp": peer(d)}, device_id_type=MESH)
    for dz, dy in NEAR[1:]:
        for d in range(MP):
            pl.semaphore_signal(barrier, inc=1, device_id={"node": node(dz, dy), "mp": peer(d)}, device_id_type=MESH)
    for d in range(2, NZ - 1):
        pl.semaphore_signal(barrier, inc=1, device_id={"node": node(d, 0)}, device_id_type=MESH)
    lane = lax.broadcasted_iota(jnp.int32, (1, 128), 1)
    row = jnp.zeros((1, 128), jnp.int32)
    for level in range(LEVELS):
        row = jnp.where(lane == level, len_s[level], row)
    for level in range(LEVELS - 1):
        row = jnp.where(lane == LEVELS + level, par_s[level], row)
    meta[n] = row
    for kv in range(2):
        arrived(sources[kv], loc_sem.at[kv])
    pl.semaphore_wait(barrier, (MP - 1) + (len(NEAR) - 1) * MP + (NZ - 3))

    for kv, near in HOPS:
        dz, dy = NEAR[near]
        dst = gathered[kv].at[n, own_tok]
        for d in range(1, MP):
            p = peer(d)
            to_any(sources[kv].at[own_class, :, pl.ds(p * HD, HD)], dst, HOP, hop_rs.at[kv, near], node(dz, dy), p)
        src = sources[kv].at[own_class, :, own_lanes]
        if near:
            to_node(src, dst, HOP, hop_rs.at[kv, near], node(dz, dy))
        else:
            local(src, dst, hop_rs.at[kv, near])
    for d in range(1, NY):
        to_node(meta.at[n], meta.at[n], META, meta_rs.at[0], node(0, d))
    for kv in range(2):
        for d in range(1, MP):
            p = peer(d)
            to_mp(sources[kv].at[:, :, pl.ds(p * HD, HD)], kvl.at[kv, :, own_tok], SHARE, a2a_rs.at[kv], p)
        local(sources[kv].at[:, :, own_lanes], kvl.at[kv, :, own_tok], a2a_rs.at[kv])

    def hop_wait(kv, near):
        dz, dy = NEAR[near]
        arrived(gathered[kv].at[node(-dz, -dy)], hop_rs.at[kv, near])

    def piece(slot, col):
        return gathered[VALUE if col == 4 else KEY].at[slot]

    def ag_z(col, direction, s):
        sign = 1 if direction == 0 else -1
        src = piece(node(-sign * (s - 1), 0 if col == 4 else col), col)
        to_node(src, src, GATHER, agz_rs.at[col, direction, s], node(sign, 0))

    def ag_z_wait(col, direction, s):
        if col == 4 and s == 1:
            hop_wait(VALUE, 4 + direction)
            return
        sign = 1 if direction == 0 else -1
        dst = piece(node(-sign * s, 0 if col == 4 else col), col)
        arrived(dst, agz_rs.at[col, direction, s])

    def ag_y(t):
        src = piece(node(t, 0), 4)
        for d in (2, 1, 3):
            to_node(src, src, GATHER, agy_rs.at[0], node(0, d))

    def gather_start():
        hop_wait(KEY, 0)
        for direction in range(2):
            ag_z(0, direction, 1)
        hop_wait(VALUE, 0)
        ag_y(0)
        for d in (1, 3, 2):
            hop_wait(KEY, d)
            for direction in range(2):
                ag_z(NY - d, direction, 1)

    def gather_round(s):
        for col in (4, 0, 3, 1, 2):
            for direction in range(2):
                reach = REACH[col][direction]
                if s > reach:
                    continue
                ag_z_wait(col, direction, s)
                if s < reach:
                    ag_z(col, direction, s + 1)
                if col == 4:
                    ag_y((-s if direction == 0 else s) % NZ)

    def gather_end():
        arrived(vg.at[pl.ds(0, (NY - 1) * NZ)], agy_rs.at[0])

    def parent(a, slot):
        return meta_s[slot, 0, LEVELS + a]

    def length(level, slot):
        return meta_s[slot, 0, level]

    def limits(level):
        return [length(a, chains[level][a]) for a in range(level)] + [length(level, n)]

    def fill_context(level, kv, dst):
        first, _ = context(level)
        for a in range(level):
            dst[first + a * SEG:first + (a + 1) * SEG, :] = gathered[kv][chains[level][a]]
        dst[first + level * SEG:first + (level + 1) * SEG, :] = kvl[kv, level]

    def live_rows(level):
        return lax.broadcasted_iota(jnp.int32, (SEG, HD), 0) < length(level, n)

    def probabilities(level):
        first, ctx = context(level)
        fill_context(level, KEY, kc)
        live = live_rows(level)
        for g in range(GROUPS):
            rows = slice(g * SEG, (g + 1) * SEG)
            dos[level, rows, :] = jnp.where(live, dos[level, rows, :], jnp.zeros((), BF16))
        span = slice(first, first + ctx)
        st[span, :] = dot(kc[span, :], qs[level], 1, 1)
        limit = limits(level)
        peak = jnp.full((8, QR), -jnp.inf, F32)
        for r in range(0, ctx, CH):
            b, off = r // SEG, r % SEG
            place = lax.broadcasted_iota(jnp.int32, (CH, QR), 0) + off
            ok = place < limit[b]
            if b == level:
                ok = ok & (place <= (lax.broadcasted_iota(jnp.int32, (CH, QR), 1) & (SEG - 1)))
            s = jnp.where(ok, st[first + r:first + r + CH, :], -jnp.inf)
            st[first + r:first + r + CH, :] = s
            for i in range(0, CH, 8):
                peak = jnp.maximum(peak, s[i:i + 8, :])
        peak = jnp.max(peak, axis=0, keepdims=True)
        total = jnp.zeros((8, QR), F32)
        for r in range(first, first + ctx, CH):
            e = jnp.exp2((st[r:r + CH, :] - peak) * EXP2_SCALE)
            st[r:r + CH, :] = e
            for i in range(0, CH, 8):
                total = total + e[i:i + 8, :]
        inv = 1.0 / jnp.sum(total, axis=0, keepdims=True)
        for r in range(first, first + ctx, CH):
            p = st[r:r + CH, :] * inv
            st[r:r + CH, :] = p
            plow[r:r + CH, :] = p.astype(BF16)
        term[VALUE, span, :] = dot(plow[span, :], dos[level], 1, 0)

    def score_grads(level):
        first, ctx = context(level)
        span = slice(first, first + ctx)
        fill_context(level, VALUE, vc)
        dp[:ctx, :] = dot(vc[span, :], dos[level], 1, 1)
        inner = jnp.zeros((8, QR), F32)
        for r in range(0, ctx, CH):
            prod = st[first + r:first + r + CH, :] * dp[r:r + CH, :]
            for i in range(0, CH, 8):
                inner = inner + prod[i:i + 8, :]
        inner = jnp.sum(inner, axis=0, keepdims=True)
        for r in range(0, ctx, CH):
            g = st[first + r:first + r + CH, :] * (dp[r:r + CH, :] - inner)
            dsl[first + r:first + r + CH, :] = g.astype(BF16)
        term[KEY, span, :] = dot(dsl[span, :], qs[level], 1, 0) * SCALE

    def outputs(level):
        first, ctx = context(level)
        span = slice(first, first + ctx)
        live = live_rows(level)
        out_t = dot(vc[span, :], plow[span, :], 0, 0)
        gq_t = dot(kc[span, :], dsl[span, :], 0, 0) * SCALE
        for g in range(GROUPS):
            cols = slice(g * SEG, (g + 1) * SEG)
            att_v[level, :, cols] = jnp.where(live, jnp.transpose(out_t[:, cols]), 0.0).astype(BF16)
            gq_v[level, :, cols] = jnp.transpose(gq_t[:, cols]).astype(BF16)
        for i, (src, dst) in enumerate(((att_v, att_hbm), (gq_v, gq_hbm))):
            local(src.at[level], dst.at[level], loc_sem.at[4 + i])

    def term_sums(kv):
        for a in range(LEVELS - 1):
            names = list(range(a + 1, LEVELS))
            for bits in range(1 << len(names)):
                slot = kv * SETS + a * 8 + (bits << a)
                for r in range(0, SEG, CH):
                    acc = None
                    for i, level in enumerate(names):
                        if bits >> i & 1:
                            start = context(level)[0] + a * SEG + r
                            x = term[kv, start:start + CH, :]
                            acc = x if acc is None else acc + x
                    if acc is None:
                        acc = jnp.zeros((CH, HD), F32)
                    cbuf[slot, r:r + CH, :] = acc.astype(BF16)

    def own_part(target, col):
        return cbuf[(VALUE if col == 4 else KEY) * SETS + set_s[target]].astype(F32)

    def spread(t):
        for d in (2, 1, 3):
            sy[t, d - 1] = own_part(node(t, d), 4).astype(BF16)
            to_node(sy.at[t, d - 1], ry.at[t, d - 1], SCATTER, rsy_rs.at[t], node(0, d))

    def total_b(t):
        acc = own_part(node(t, 0), 4)
        arrived(ry.at[t], rsy_rs.at[t])
        for d in range(1, NY):
            acc = acc + ry[t, d - 1].astype(F32)
        return acc

    def rs_z(col, direction, t, first):
        src = rz0.at[col, direction] if first else rz.at[col, direction, t]
        to_node(src, rz.at[col, direction, t - 1], SCATTER, rsz_rs.at[col, direction, t - 1],
                node(1 if direction == 0 else -1, 0))

    def rs_z_wait(col, direction, t):
        arrived(rz.at[col, direction, t], rsz_rs.at[col, direction, t])

    def last_hop(kv, near, acc):
        dz, dy = NEAR[near]
        last[kv, near] = acc.astype(BF16)
        dst = got.at[kv, near, m]
        for d in range(1, MP):
            p = peer(d)
            to_any(last.at[kv, near, pl.ds(p * TOK, TOK)], dst, LAST, end_rs.at[kv, near], node(dz, dy), p)
        src = last.at[kv, near, own_tok]
        if near:
            to_node(src, dst, LAST, end_rs.at[kv, near], node(dz, dy))
        else:
            local(src, dst, end_rs.at[kv, near])

    def last_sum(kv):
        nears = [near for k, near in HOPS if k == kv]
        for near in nears:
            arrived(got.at[kv, near], end_rs.at[kv, near])
        for head in range(MP):
            acc = sum(got[kv, near, head].astype(F32) for near in nears)
            rows_out[kv, :, head * HD:(head + 1) * HD] = acc.astype(BF16)
        local(rows_out.at[kv], results[kv].at[own_class], loc_sem.at[6])

    def chain(col, step):
        for direction in range(2):
            t = REACH[col][direction] - step
            if t < 0 or (col == 4 and t == 0):
                continue
            if step > 0:
                rs_z_wait(col, direction, t)
            if t == 0:
                continue
            rel = t if direction == 0 else -t
            acc = total_b(rel % NZ) if col == 4 else own_part(node(rel, col), col)
            if step > 0:
                acc = acc + rz[col, direction, t].astype(F32)
            if col == 4 and t == 1:
                last_hop(VALUE, 4 + direction, acc)
                continue
            if step == 0:
                rz0[col, direction] = acc.astype(BF16)
            else:
                rz[col, direction, t] = acc.astype(BF16)
            rs_z(col, direction, t, step == 0)

    def keys_step(step):
        for col in COLS:
            chain(col, step)

    def keys_turn():
        for col in COLS:
            acc = own_part(node(0, col), col) + rz[col, 0, 0].astype(F32) + rz[col, 1, 0].astype(F32)
            if col == 0:
                acc = acc + own_term(KEY, pl.ds(own_start(own_class), SEG))
            last_hop(KEY, col, acc)

    def values_turn():
        last_hop(VALUE, 0, total_b(0) + own_term(VALUE, pl.ds(own_start(own_class), SEG)))

    def send_back(kv, level):
        dst = results[kv].at[level, :, own_lanes]
        for d in range(1, MP):
            p = peer(d)
            to_mp(gfin.at[kv, level, pl.ds(p * TOK, TOK)], dst, BACK, back_rs.at[kv], p)
        local(gfin.at[kv, level, own_tok], dst, back_rs.at[kv])

    def own_term(kv, level_rows):
        return term[kv, level_rows, :]

    def own_start(level):
        return (level * (level + 3) // 2) * SEG

    def finish_own(kv):
        for i in range(1, LEVELS):
            level = lax.rem(own_class + i, LEVELS)
            gfin[kv, level] = own_term(kv, pl.ds(own_start(level), SEG)).astype(BF16)
            send_back(kv, level)

    gather_start()
    my_row = pl.ds(node(0, 0) - y, NY)
    arrived(meta.at[pl.ds(0, NY - 1)], meta_rs.at[0])
    for d in range(1, NZ):
        to_node(meta.at[my_row], meta.at[my_row], META, meta_rs.at[1], node(d, 0))
    gather_round(1)
    gather_round(2)
    arrived(meta.at[pl.ds(0, NODES - NY)], meta_rs.at[1])
    local(meta, meta_s, loc_sem.at[7])
    pltpu.make_async_copy(meta, meta_s, loc_sem.at[7]).wait()
    chains = []
    for level in range(LEVELS):
        links = [None] * level
        slot = n
        for a in reversed(range(level)):
            slot = parent(a, slot)
            links[a] = slot
        chains.append(links)
    for target in range(NODES):
        a = target % (LEVELS - 1)
        slot = jnp.int32(a * 8)
        for level in range(a + 1, LEVELS):
            slot = slot + (chains[level][a] == target).astype(jnp.int32) * (1 << (level - 1))
        set_s[target] = slot
    gather_round(3)
    arrived(qs, loc_sem.at[2])
    arrived(dos, loc_sem.at[3])
    for kv in range(2):
        arrived(kvl.at[kv], a2a_rs.at[kv])
    probabilities(0)
    gather_round(4)
    probabilities(3)
    probabilities(2)
    probabilities(1)
    term_sums(VALUE)
    for t in (4, 5, 3, 6):
        spread(t)
    gather_end()
    score_grads(3)
    score_grads(2)
    chain(4, 0)
    spread(2)
    spread(7)
    score_grads(1)
    term_sums(KEY)
    keys_step(0)
    chain(4, 1)
    spread(1)
    spread(0)
    outputs(3)
    keys_step(1)
    chain(4, 2)
    outputs(2)
    keys_step(2)
    chain(4, 3)
    score_grads(0)
    finish_own(VALUE)
    finish_own(KEY)
    outputs(1)
    keys_step(3)
    values_turn()
    outputs(0)
    keys_step(4)
    keys_turn()
    last_sum(VALUE)
    last_sum(KEY)
    for kv in (VALUE, KEY):
        arrived(results[kv].at[pl.ds(0, LEVELS - 1)], back_rs.at[kv])
    arrived(att_v, loc_sem.at[4])
    arrived(gq_v, loc_sem.at[5])
    arrived(rows_out, loc_sem.at[6])
    units = {HOP: len(HOPS) * MP - 2, SHARE: 2 * (MP - 1) * LEVELS, GATHER: 57 * MP, SCATTER: 57 * MP,
             LAST: len(HOPS) * MP - 2, BACK: 2 * (MP - 1) * (LEVELS - 1)}
    for kind, count in units.items():
        arrived(sent.at[pl.ds(0, count)], send_sem.at[kind])
    arrived(meta.at[pl.ds(0, NODES - 1)], send_sem.at[META])


def per_device(queries, keys, values, grad_out, lengths, parents):
    hbm = pl.BlockSpec(memory_space=pltpu.HBM)
    smem = pl.BlockSpec(memory_space=pltpu.SMEM)
    dma = pltpu.SemaphoreType.DMA
    vm = pltpu.VMEM
    ctx = LEVELS * SEG
    block = (SEG, HD)
    results = pl.pallas_call(
        kernel,
        out_shape=tuple(jax.ShapeDtypeStruct(x.shape, BF16) for x in (queries, queries, keys, keys)),
        in_specs=[hbm, hbm, hbm, hbm, smem, smem],
        out_specs=(hbm,) * 4,
        scratch_shapes=[
            vm((LEVELS, TOK, MP * HD), BF16), vm((LEVELS, TOK, MP * HD), BF16),
            vm((LEVELS, QR, HD), BF16), vm((LEVELS, QR, HD), BF16),
            vm((2, LEVELS, SEG, HD), BF16), vm((NODES, SEG, HD), BF16), vm((NODES, SEG, HD), BF16),
            vm((NODES, 1, 128), jnp.int32), pltpu.SMEM((NODES, 1, 128), jnp.int32), pltpu.SMEM((NODES,), jnp.int32),
            vm((CTX_ROWS, HD), BF16), vm((CTX_ROWS, HD), BF16),
            vm((CTX_ROWS, QR), F32), vm((ctx, QR), F32), vm((CTX_ROWS, QR), BF16), vm((CTX_ROWS, QR), BF16),
            vm((LEVELS, SEG, QR), BF16), vm((LEVELS, SEG, QR), BF16),
            vm((2, CTX_ROWS, HD), F32), vm((2 * SETS, SEG, HD), BF16), vm((2, LEVELS, SEG, HD), BF16),
            vm((5, 2, 4) + block, BF16), vm((5, 2) + block, BF16),
            vm((NZ, NY - 1) + block, BF16), vm((NZ, NY - 1) + block, BF16),
            vm((2, len(NEAR)) + block, BF16), vm((2, len(NEAR), MP, TOK, HD), BF16), vm((2, TOK, MP * HD), BF16),
            vm((57 * MP, TOK, HD), BF16),
            dma((8,)), dma((7,)), dma((2,)), dma((2,)), dma((2, len(NEAR))), dma((5, 2, 5)), dma((1,)),
            dma((5, 2, 4)), dma((NZ,)), dma((2, len(NEAR))), dma((2,)),
        ],
        compiler_params=pltpu.CompilerParams(collective_id=0, has_side_effects=True, vmem_limit_bytes=60 << 20),
        name="tree_attention",
    )(queries, keys, values, grad_out, lengths.reshape(LEVELS), parents.reshape(LEVELS - 1))
    return tuple(results)


def solution(mesh):
    placed = (
        P(None, "node", "mp"),
        P(None, ("node", "mp"), None),
        P(None, ("node", "mp"), None),
        P(None, "node", "mp"),
        P(None, "node"),
        P(None, "node"),
    )
    return jax.shard_map(
        per_device,
        mesh=mesh,
        in_specs=placed,
        out_specs=(
            P(None, "node", "mp"),
            P(None, "node", "mp"),
            P(None, ("node", "mp"), None),
            P(None, ("node", "mp"), None),
        ),
        check_vma=False,
    )
```

```python
import functools
import math

import jax
import jax.numpy as jnp
from jax import lax
from jax.experimental import pallas as pl
from jax.experimental.pallas import tpu as pltpu
from jax.sharding import PartitionSpec as P

HD = 128
SEG = 128
NZ, NY = 8, 4
NODES = NZ * NY
MP = 8
LEVELS = 4
GROUPS = 5
QR = GROUPS * SEG
TOK = SEG // MP
CTX_ROWS = SEG * LEVELS * (LEVELS + 1) // 2
SETS = 24
F32 = jnp.float32
BF16 = jnp.bfloat16
MESH = pl.DeviceIdType.MESH
SCALE = 1.0 / math.sqrt(HD)
EXP2_SCALE = SCALE * math.log2(math.e)
CH = 32
KEY, VALUE = 0, 1
HOP, META, SHARE, GATHER, SCATTER, LAST, BACK = range(7)
REACH = [(4, 3), (3, 4), (4, 3), (3, 4), (4, 3)]
COLS = (2, 1, 3, 0)
NEAR = [(0, 0), (0, 1), (0, 2), (0, 3), (1, 0), (-1, 0)]
ENDS = {VALUE: (0, 1, 2, 3), KEY: (0, 4, 5)}
HOPS = [(KEY, 2), (VALUE, 4), (VALUE, 5), (KEY, 1), (KEY, 3), (KEY, 0), (VALUE, 0)]


def dot(a, b, ca, cb):
    return lax.dot_general(a, b, (((ca,), (cb,)), ((), ())), preferred_element_type=F32)


def context(level):
    first = SEG * level * (level + 1) // 2
    return first, (level + 1) * SEG


def kernel(q_hbm, k_hbm, v_hbm, do_hbm, len_s, par_s,
           att_hbm, gq_hbm, gk_o, gv_o,
           ksrc, vsrc, qs, dos, kvl, kg, vg, meta, meta_s, set_s,
           kc, vc, st, dp, plow, dsl, att_v, gq_v, term, cbuf, gfin,
           rz, rz0, ry, sy, last, got, rows_out,
           sent, loc_sem, send_sem, meta_rs, a2a_rs, hop_rs, agz_rs, agy_rs, rsz_rs, rsy_rs, end_rs, back_rs):
    n = lax.axis_index("node")
    m = lax.axis_index("mp")
    z = n >> 2
    y = n & (NY - 1)
    own_class = lax.rem(n, LEVELS - 1)
    sources = (ksrc, vsrc)
    results = (gk_o, gv_o)
    gathered = (kg, vg)

    def node(dz, dy):
        up = ((z + dz) & (NZ - 1)) << 2 if dz % NZ else z << 2
        return up | ((y + dy) & (NY - 1) if dy % NY else y)

    def peer(d):
        return (m + d) & (MP - 1)

    def remote(src, dst, ss, rs, to):
        pltpu.make_async_remote_copy(src_ref=src, dst_ref=dst, send_sem=send_sem.at[ss], recv_sem=rs,
                                     device_id=to, device_id_type=MESH).start()

    def to_node(src, dst, ss, rs, target):
        remote(src, dst, ss, rs, {"node": target})

    def to_mp(src, dst, ss, rs, target):
        remote(src, dst, ss, rs, {"mp": target})

    def to_any(src, dst, ss, rs, target, p):
        remote(src, dst, ss, rs, {"node": target, "mp": p})

    def arrived(ref, sem):
        pltpu.make_async_copy(ref, ref, sem).wait()

    def local(src, dst, sem):
        pltpu.make_async_copy(src, dst, sem).start()

    own_tok = pl.ds(m * TOK, TOK)
    own_lanes = pl.ds(m * HD, HD)
    for kv, src in enumerate((k_hbm, v_hbm)):
        local(src, sources[kv], loc_sem.at[kv])
    for g in range(GROUPS):
        lanes = pl.ds(g * HD, HD)
        for i, (src, dst) in enumerate(((q_hbm, qs), (do_hbm, dos))):
            local(src.at[:, :, lanes], dst.at[:, pl.ds(g * SEG, SEG), :], loc_sem.at[2 + i])

    barrier = pltpu.get_barrier_semaphore()
    for d in range(1, MP):
        pl.semaphore_signal(barrier, inc=1, device_id={"mp": peer(d)}, device_id_type=MESH)
    for dz, dy in NEAR[1:]:
        for d in range(MP):
            pl.semaphore_signal(barrier, inc=1, device_id={"node": node(dz, dy), "mp": peer(d)}, device_id_type=MESH)
    for d in range(2, NZ - 1):
        pl.semaphore_signal(barrier, inc=1, device_id={"node": node(d, 0)}, device_id_type=MESH)
    lane = lax.broadcasted_iota(jnp.int32, (1, 128), 1)
    row = jnp.zeros((1, 128), jnp.int32)
    for level in range(LEVELS):
        row = jnp.where(lane == level, len_s[level], row)
    for level in range(LEVELS - 1):
        row = jnp.where(lane == LEVELS + level, par_s[level], row)
    meta[n] = row
    for kv in range(2):
        arrived(sources[kv], loc_sem.at[kv])
    pl.semaphore_wait(barrier, (MP - 1) + (len(NEAR) - 1) * MP + (NZ - 3))

    for kv, near in HOPS:
        dz, dy = NEAR[near]
        dst = gathered[kv].at[n, own_tok]
        for d in range(1, MP):
            p = peer(d)
            to_any(sources[kv].at[own_class, :, pl.ds(p * HD, HD)], dst, HOP, hop_rs.at[kv, near], node(dz, dy), p)
        src = sources[kv].at[own_class, :, own_lanes]
        if near:
            to_node(src, dst, HOP, hop_rs.at[kv, near], node(dz, dy))
        else:
            local(src, dst, hop_rs.at[kv, near])
    for d in range(1, NY):
        to_node(meta.at[n], meta.at[n], META, meta_rs.at[0], node(0, d))
    for kv in range(2):
        for d in range(1, MP):
            p = peer(d)
            to_mp(sources[kv].at[:, :, pl.ds(p * HD, HD)], kvl.at[kv, :, own_tok], SHARE, a2a_rs.at[kv], p)
        local(sources[kv].at[:, :, own_lanes], kvl.at[kv, :, own_tok], a2a_rs.at[kv])

    def hop_wait(kv, near):
        dz, dy = NEAR[near]
        arrived(gathered[kv].at[node(-dz, -dy)], hop_rs.at[kv, near])

    def piece(slot, col):
        return gathered[VALUE if col == 4 else KEY].at[slot]

    def ag_z(col, direction, s):
        sign = 1 if direction == 0 else -1
        src = piece(node(-sign * (s - 1), 0 if col == 4 else col), col)
        to_node(src, src, GATHER, agz_rs.at[col, direction, s], node(sign, 0))

    def ag_z_wait(col, direction, s):
        if col == 4 and s == 1:
            hop_wait(VALUE, 4 + direction)
            return
        sign = 1 if direction == 0 else -1
        dst = piece(node(-sign * s, 0 if col == 4 else col), col)
        arrived(dst, agz_rs.at[col, direction, s])

    def ag_y(t):
        src = piece(node(t, 0), 4)
        for d in (2, 1, 3):
            to_node(src, src, GATHER, agy_rs.at[0], node(0, d))

    def gather_start():
        hop_wait(KEY, 0)
        for direction in range(2):
            ag_z(0, direction, 1)
        hop_wait(VALUE, 0)
        ag_y(0)
        for d in (1, 3, 2):
            hop_wait(KEY, d)
            for direction in range(2):
                ag_z(NY - d, direction, 1)

    def gather_round(s):
        for col in (4, 0, 3, 1, 2):
            for direction in range(2):
                reach = REACH[col][direction]
                if s > reach:
                    continue
                ag_z_wait(col, direction, s)
                if s < reach:
                    ag_z(col, direction, s + 1)
                if col == 4:
                    ag_y((-s if direction == 0 else s) % NZ)

    def gather_end():
        arrived(vg.at[pl.ds(0, (NY - 1) * NZ)], agy_rs.at[0])

    def parent(a, slot):
        return meta_s[slot, 0, LEVELS + a]

    def length(level, slot):
        return meta_s[slot, 0, level]

    def limits(level):
        return [length(a, chains[level][a]) for a in range(level)] + [length(level, n)]

    def fill_context(level, kv, dst):
        first, _ = context(level)
        for a in range(level):
            dst[first + a * SEG:first + (a + 1) * SEG, :] = gathered[kv][chains[level][a]]
        dst[first + level * SEG:first + (level + 1) * SEG, :] = kvl[kv, level]

    def live_rows(level):
        return lax.broadcasted_iota(jnp.int32, (SEG, HD), 0) < length(level, n)

    def probabilities(level):
        first, ctx = context(level)
        fill_context(level, KEY, kc)
        live = live_rows(level)
        for g in range(GROUPS):
            rows = slice(g * SEG, (g + 1) * SEG)
            dos[level, rows, :] = jnp.where(live, dos[level, rows, :], jnp.zeros((), BF16))
        span = slice(first, first + ctx)
        st[span, :] = dot(kc[span, :], qs[level], 1, 1)
        limit = limits(level)
        peak = jnp.full((8, QR), -jnp.inf, F32)
        for r in range(0, ctx, CH):
            b, off = r // SEG, r % SEG
            place = lax.broadcasted_iota(jnp.int32, (CH, QR), 0) + off
            ok = place < limit[b]
            if b == level:
                ok = ok & (place <= (lax.broadcasted_iota(jnp.int32, (CH, QR), 1) & (SEG - 1)))
            s = jnp.where(ok, st[first + r:first + r + CH, :], -jnp.inf)
            st[first + r:first + r + CH, :] = s
            for i in range(0, CH, 8):
                peak = jnp.maximum(peak, s[i:i + 8, :])
        peak = jnp.max(peak, axis=0, keepdims=True)
        total = jnp.zeros((8, QR), F32)
        for r in range(first, first + ctx, CH):
            e = jnp.exp2((st[r:r + CH, :] - peak) * EXP2_SCALE)
            st[r:r + CH, :] = e
            for i in range(0, CH, 8):
                total = total + e[i:i + 8, :]
        inv = 1.0 / jnp.sum(total, axis=0, keepdims=True)
        for r in range(first, first + ctx, CH):
            p = st[r:r + CH, :] * inv
            st[r:r + CH, :] = p
            plow[r:r + CH, :] = p.astype(BF16)
        term[VALUE, span, :] = dot(plow[span, :], dos[level], 1, 0)

    def score_grads(level):
        first, ctx = context(level)
        span = slice(first, first + ctx)
        fill_context(level, VALUE, vc)
        dp[:ctx, :] = dot(vc[span, :], dos[level], 1, 1)
        inner = jnp.zeros((8, QR), F32)
        for r in range(0, ctx, CH):
            prod = st[first + r:first + r + CH, :] * dp[r:r + CH, :]
            for i in range(0, CH, 8):
                inner = inner + prod[i:i + 8, :]
        inner = jnp.sum(inner, axis=0, keepdims=True)
        for r in range(0, ctx, CH):
            g = st[first + r:first + r + CH, :] * (dp[r:r + CH, :] - inner)
            dsl[first + r:first + r + CH, :] = g.astype(BF16)
        term[KEY, span, :] = dot(dsl[span, :], qs[level], 1, 0) * SCALE

    def outputs(level):
        first, ctx = context(level)
        span = slice(first, first + ctx)
        live = live_rows(level)
        out_t = dot(vc[span, :], plow[span, :], 0, 0)
        gq_t = dot(kc[span, :], dsl[span, :], 0, 0) * SCALE
        for g in range(GROUPS):
            cols = slice(g * SEG, (g + 1) * SEG)
            att_v[level, :, cols] = jnp.where(live, jnp.transpose(out_t[:, cols]), 0.0).astype(BF16)
            gq_v[level, :, cols] = jnp.transpose(gq_t[:, cols]).astype(BF16)
        for i, (src, dst) in enumerate(((att_v, att_hbm), (gq_v, gq_hbm))):
            local(src.at[level], dst.at[level], loc_sem.at[4 + i])

    def term_sums(kv):
        for a in range(LEVELS - 1):
            names = list(range(a + 1, LEVELS))
            for bits in range(1 << len(names)):
                slot = kv * SETS + a * 8 + (bits << a)
                for r in range(0, SEG, CH):
                    acc = None
                    for i, level in enumerate(names):
                        if bits >> i & 1:
                            start = context(level)[0] + a * SEG + r
                            x = term[kv, start:start + CH, :]
                            acc = x if acc is None else acc + x
                    if acc is None:
                        acc = jnp.zeros((CH, HD), F32)
                    cbuf[slot, r:r + CH, :] = acc.astype(BF16)

    def own_part(target, col):
        return cbuf[(KEY if col == 4 else VALUE) * SETS + set_s[target]].astype(F32)

    def spread(t):
        for d in (2, 1, 3):
            sy[t, d - 1] = own_part(node(t, d), 4).astype(BF16)
            to_node(sy.at[t, d - 1], ry.at[t, d - 1], SCATTER, rsy_rs.at[t], node(0, d))

    def total_b(t):
        acc = own_part(node(t, 0), 4)
        arrived(ry.at[t], rsy_rs.at[t])
        for d in range(1, NY):
            acc = acc + ry[t, d - 1].astype(F32)
        return acc

    def rs_z(col, direction, t, first):
        src = rz0.at[col, direction] if first else rz.at[col, direction, t]
        to_node(src, rz.at[col, direction, t - 1], SCATTER, rsz_rs.at[col, direction, t - 1],
                node(1 if direction == 0 else -1, 0))

    def rs_z_wait(col, direction, t):
        arrived(rz.at[col, direction, t], rsz_rs.at[col, direction, t])

    def last_hop(kv, near, acc):
        dz, dy = NEAR[near]
        last[kv, near] = acc.astype(BF16)
        dst = got.at[kv, near, m]
        for d in range(1, MP):
            p = peer(d)
            to_any(last.at[kv, near, pl.ds(p * TOK, TOK)], dst, LAST, end_rs.at[kv, near], node(dz, dy), p)
        src = last.at[kv, near, own_tok]
        if near:
            to_node(src, dst, LAST, end_rs.at[kv, near], node(dz, dy))
        else:
            local(src, dst, end_rs.at[kv, near])

    def last_sum(kv):
        nears = ENDS[kv]
        for near in nears:
            arrived(got.at[kv, near], end_rs.at[kv, near])
        for head in range(MP):
            acc = sum(got[kv, near, head].astype(F32) for near in nears)
            rows_out[kv, :, head * HD:(head + 1) * HD] = acc.astype(BF16)
        local(rows_out.at[kv], results[kv].at[own_class], loc_sem.at[6])

    def chain(col, step):
        for direction in range(2):
            t = REACH[col][direction] - step
            if t < 0 or (col == 4 and t == 0):
                continue
            if step > 0:
                rs_z_wait(col, direction, t)
            if t == 0:
                continue
            rel = t if direction == 0 else -t
            acc = total_b(rel % NZ) if col == 4 else own_part(node(rel, col), col)
            if step > 0:
                acc = acc + rz[col, direction, t].astype(F32)
            if col == 4 and t == 1:
                last_hop(KEY, 4 + direction, acc)
                continue
            if step == 0:
                rz0[col, direction] = acc.astype(BF16)
            else:
                rz[col, direction, t] = acc.astype(BF16)
            rs_z(col, direction, t, step == 0)

    def ring_step(step):
        for col in COLS:
            chain(col, step)

    def ring_turn():
        for col in COLS:
            acc = own_part(node(0, col), col) + rz[col, 0, 0].astype(F32) + rz[col, 1, 0].astype(F32)
            if col == 0:
                acc = acc + own_term(VALUE, pl.ds(own_start(own_class), SEG))
            last_hop(VALUE, col, acc)

    def spread_turn():
        last_hop(KEY, 0, total_b(0) + own_term(KEY, pl.ds(own_start(own_class), SEG)))

    def send_back(kv, level):
        dst = results[kv].at[level, :, own_lanes]
        for d in range(1, MP):
            p = peer(d)
            to_mp(gfin.at[kv, level, pl.ds(p * TOK, TOK)], dst, BACK, back_rs.at[kv], p)
        local(gfin.at[kv, level, own_tok], dst, back_rs.at[kv])

    def own_term(kv, level_rows):
        return term[kv, level_rows, :]

    def own_start(level):
        return (level * (level + 3) // 2) * SEG

    def finish_own(kv):
        for i in range(1, LEVELS):
            level = lax.rem(own_class + i, LEVELS)
            gfin[kv, level] = own_term(kv, pl.ds(own_start(level), SEG)).astype(BF16)
            send_back(kv, level)

    gather_start()
    my_row = pl.ds(node(0, 0) - y, NY)
    arrived(meta.at[pl.ds(0, NY - 1)], meta_rs.at[0])
    for d in range(1, NZ):
        to_node(meta.at[my_row], meta.at[my_row], META, meta_rs.at[1], node(d, 0))
    gather_round(1)
    gather_round(2)
    arrived(meta.at[pl.ds(0, NODES - NY)], meta_rs.at[1])
    local(meta, meta_s, loc_sem.at[7])
    pltpu.make_async_copy(meta, meta_s, loc_sem.at[7]).wait()
    chains = []
    for level in range(LEVELS):
        links = [None] * level
        slot = n
        for a in reversed(range(level)):
            slot = parent(a, slot)
            links[a] = slot
        chains.append(links)
    for target in range(NODES):
        a = target % (LEVELS - 1)
        slot = jnp.int32(a * 8)
        for level in range(a + 1, LEVELS):
            slot = slot + (chains[level][a] == target).astype(jnp.int32) * (1 << (level - 1))
        set_s[target] = slot
    gather_round(3)
    arrived(qs, loc_sem.at[2])
    arrived(dos, loc_sem.at[3])
    for kv in range(2):
        arrived(kvl.at[kv], a2a_rs.at[kv])
    probabilities(0)
    gather_round(4)
    probabilities(3)
    probabilities(2)
    probabilities(1)
    term_sums(VALUE)
    ring_step(0)
    gather_end()
    score_grads(3)
    score_grads(2)
    score_grads(1)
    term_sums(KEY)
    for t in (4, 5, 3, 6):
        spread(t)
    ring_step(1)
    spread(2)
    spread(7)
    finish_own(VALUE)
    chain(4, 0)
    ring_step(2)
    spread(1)
    spread(0)
    score_grads(0)
    outputs(3)
    chain(4, 1)
    ring_step(3)
    finish_own(KEY)
    outputs(2)
    chain(4, 2)
    ring_step(4)
    ring_turn()
    chain(4, 3)
    spread_turn()
    outputs(1)
    outputs(0)
    last_sum(VALUE)
    last_sum(KEY)
    for kv in (VALUE, KEY):
        arrived(results[kv].at[pl.ds(0, LEVELS - 1)], back_rs.at[kv])
    arrived(att_v, loc_sem.at[4])
    arrived(gq_v, loc_sem.at[5])
    arrived(rows_out, loc_sem.at[6])
    units = {HOP: len(HOPS) * MP - 2, SHARE: 2 * (MP - 1) * LEVELS, GATHER: 57 * MP, SCATTER: 57 * MP,
             LAST: len(HOPS) * MP - 2, BACK: 2 * (MP - 1) * (LEVELS - 1)}
    for kind, count in units.items():
        arrived(sent.at[pl.ds(0, count)], send_sem.at[kind])
    arrived(meta.at[pl.ds(0, NODES - 1)], send_sem.at[META])


def store(pieces, *refs):
    src, dst, buf, (load_sem, store_sem) = refs[:4], refs[4:8], refs[8:12], refs[12:]

    def part(arrays, piece):
        i, level = piece
        return arrays[i] if level is None else arrays[i].at[level]

    loads = [pltpu.make_async_copy(part(src, p), part(buf, p), load_sem.at[k]) for k, p in enumerate(pieces)]
    stores = [pltpu.make_async_copy(part(buf, p), part(dst, p), store_sem.at[k]) for k, p in enumerate(pieces)]
    for c in loads:
        c.start()
    for a, b in zip(loads, stores):
        a.wait()
        b.start()
    for c in stores:
        c.wait()


def per_device(queries, keys, values, grad_out, lengths, parents):
    hbm = pl.BlockSpec(memory_space=pltpu.HBM)
    smem = pl.BlockSpec(memory_space=pltpu.SMEM)
    dma = pltpu.SemaphoreType.DMA
    vm = pltpu.VMEM
    ctx = LEVELS * SEG
    block = (SEG, HD)
    results = pl.pallas_call(
        kernel,
        out_shape=tuple(jax.ShapeDtypeStruct(x.shape, BF16) for x in (queries, queries, keys, keys)),
        in_specs=[hbm, hbm, hbm, hbm, smem, smem],
        out_specs=(hbm,) * 4,
        scratch_shapes=[
            vm((LEVELS, TOK, MP * HD), BF16), vm((LEVELS, TOK, MP * HD), BF16),
            vm((LEVELS, QR, HD), BF16), vm((LEVELS, QR, HD), BF16),
            vm((2, LEVELS, SEG, HD), BF16), vm((NODES, SEG, HD), BF16), vm((NODES, SEG, HD), BF16),
            vm((NODES, 1, 128), jnp.int32), pltpu.SMEM((NODES, 1, 128), jnp.int32), pltpu.SMEM((NODES,), jnp.int32),
            vm((CTX_ROWS, HD), BF16), vm((CTX_ROWS, HD), BF16),
            vm((CTX_ROWS, QR), F32), vm((ctx, QR), F32), vm((CTX_ROWS, QR), BF16), vm((CTX_ROWS, QR), BF16),
            vm((LEVELS, SEG, QR), BF16), vm((LEVELS, SEG, QR), BF16),
            vm((2, CTX_ROWS, HD), F32), vm((2 * SETS, SEG, HD), BF16), vm((2, LEVELS, SEG, HD), BF16),
            vm((5, 2, 4) + block, BF16), vm((5, 2) + block, BF16),
            vm((NZ, NY - 1) + block, BF16), vm((NZ, NY - 1) + block, BF16),
            vm((2, len(NEAR)) + block, BF16), vm((2, len(NEAR), MP, TOK, HD), BF16), vm((2, TOK, MP * HD), BF16),
            vm((57 * MP, TOK, HD), BF16),
            dma((8,)), dma((7,)), dma((2,)), dma((2,)), dma((2, len(NEAR))), dma((5, 2, 5)), dma((1,)),
            dma((5, 2, 4)), dma((NZ,)), dma((2, len(NEAR))), dma((2,)),
        ],
        compiler_params=pltpu.CompilerParams(collective_id=0, has_side_effects=True, vmem_limit_bytes=60 << 20),
        name="tree_attention",
    )(queries, keys, values, grad_out, lengths.reshape(LEVELS), parents.reshape(LEVELS - 1))
    pieces = [(i, level) for i in range(2) for level in range(LEVELS)] + [(2, None), (3, None)]
    return tuple(pl.pallas_call(
        functools.partial(store, pieces),
        out_shape=tuple(jax.ShapeDtypeStruct(x.shape, BF16) for x in results),
        in_specs=[hbm] * 4,
        out_specs=(hbm,) * 4,
        scratch_shapes=[vm(x.shape, BF16) for x in results] + [dma((len(pieces),)), dma((len(pieces),))],
        name="store",
    )(*results))


def solution(mesh):
    placed = (
        P(None, "node", "mp"),
        P(None, ("node", "mp"), None),
        P(None, ("node", "mp"), None),
        P(None, "node", "mp"),
        P(None, "node"),
        P(None, "node"),
    )
    return jax.shard_map(
        per_device,
        mesh=mesh,
        in_specs=placed,
        out_specs=(
            P(None, "node", "mp"),
            P(None, "node", "mp"),
            P(None, ("node", "mp"), None),
            P(None, ("node", "mp"), None),
        ),
        check_vma=False,
    )
```

```python
import functools
import math

import jax
import jax.numpy as jnp
from jax import lax
from jax.experimental import pallas as pl
from jax.experimental.pallas import tpu as pltpu
from jax.sharding import PartitionSpec as P

HD = 128
SEG = 128
NZ, NY = 8, 4
NODES = NZ * NY
MP = 8
LEVELS = 4
GROUPS = 5
QR = GROUPS * SEG
TOK = SEG // MP
CTX_ROWS = SEG * LEVELS * (LEVELS + 1) // 2
SETS = 24
F32 = jnp.float32
BF16 = jnp.bfloat16
MESH = pl.DeviceIdType.MESH
SCALE = 1.0 / math.sqrt(HD)
EXP2_SCALE = SCALE * math.log2(math.e)
CH = 32
KEY, VALUE = 0, 1
HOP, META, SHARE, GATHER, SCATTER, LAST, BACK = range(7)
REACH = [(4, 3), (3, 4), (4, 3), (3, 4), (4, 3)]
COLS = (2, 1, 3, 0)
STEPS = [(c, i, s) for c in range(5) for i in range(2) for s in range(REACH[c][i])]
AGZ = {(c, i, s + 1): k for k, (c, i, s) in enumerate(x for x in STEPS if x[0] < 4 or x[2])}
RSZ = {x: k for k, x in enumerate(x for x in STEPS if x[0] < 4 or x[2])}
NEAR = [(0, 0), (0, 1), (0, 2), (0, 3), (1, 0), (-1, 0)]
ENDS = [(VALUE, 0), (VALUE, 1), (VALUE, 2), (VALUE, 3), (KEY, 0), (KEY, 4), (KEY, 5)]
HOPS = [(KEY, 0), (VALUE, 0), (VALUE, 4), (VALUE, 5), (KEY, 1), (KEY, 3), (KEY, 2)]


def dot(a, b, ca, cb):
    return lax.dot_general(a, b, (((ca,), (cb,)), ((), ())), preferred_element_type=F32)


def context(level):
    first = SEG * level * (level + 1) // 2
    return first, (level + 1) * SEG


def kernel(q_hbm, k_hbm, v_hbm, do_hbm, len_s, par_s,
           att_hbm, gq_hbm, gk_o, gv_o,
           ksrc, vsrc, qs, dos, kvl, kg, vg, meta, meta_s, set_s,
           kc, vc, st, dp, plow, dsl, att_v, gq_v, term, cbuf, gfin,
           rz, rz0, ry, sy, last, got, rows_out,
           sent, loc_sem, send_sem, meta_rs, a2a_rs, hop_rs, agz_rs, agy_rs, rsz_rs, rsy_rs, end_rs, back_rs):
    n = lax.axis_index("node")
    m = lax.axis_index("mp")
    z = n >> 2
    y = n & (NY - 1)
    own_class = lax.rem(n, LEVELS - 1)
    sources = (ksrc, vsrc)
    results = (gk_o, gv_o)
    gathered = (kg, vg)

    def node(dz, dy):
        up = ((z + dz) & (NZ - 1)) << 2 if dz % NZ else z << 2
        return up | ((y + dy) & (NY - 1) if dy % NY else y)

    def peer(d):
        return (m + d) & (MP - 1)

    def remote(src, dst, ss, rs, to):
        pltpu.make_async_remote_copy(src_ref=src, dst_ref=dst, send_sem=send_sem.at[ss], recv_sem=rs,
                                     device_id=to, device_id_type=MESH).start()

    def to_node(src, dst, ss, rs, target):
        remote(src, dst, ss, rs, {"node": target})

    def to_mp(src, dst, ss, rs, target):
        remote(src, dst, ss, rs, {"mp": target})

    def to_any(src, dst, ss, rs, target, p):
        remote(src, dst, ss, rs, {"node": target, "mp": p})

    def arrived(ref, sem):
        pltpu.make_async_copy(ref, ref, sem).wait()

    def local(src, dst, sem):
        pltpu.make_async_copy(src, dst, sem).start()

    barrier = pltpu.get_barrier_semaphore()
    for d in (4, 3, 5, 2, 6):
        pl.semaphore_signal(barrier, inc=1, device_id={"node": node(d, 0)}, device_id_type=MESH)
    for near in (2, 1, 3, 4, 5, 0):
        for d in (4, 3, 5, 2, 6, 1, 7, 0):
            if near or d:
                pl.semaphore_signal(barrier, inc=1, device_id={"node": node(*NEAR[near]), "mp": peer(d)}, device_id_type=MESH)

    own_tok = pl.ds(m * TOK, TOK)
    own_lanes = pl.ds(m * HD, HD)
    for kv, src in enumerate((k_hbm, v_hbm)):
        local(src, sources[kv], loc_sem.at[kv])
    for g in range(GROUPS):
        lanes = pl.ds(g * HD, HD)
        for i, (src, dst) in enumerate(((q_hbm, qs), (do_hbm, dos))):
            local(src.at[:, :, lanes], dst.at[:, pl.ds(g * SEG, SEG), :], loc_sem.at[2 + i])

    lane = lax.broadcasted_iota(jnp.int32, (1, 128), 1)
    row = jnp.zeros((1, 128), jnp.int32)
    for level in range(LEVELS):
        row = jnp.where(lane == level, len_s[level], row)
    for level in range(LEVELS - 1):
        row = jnp.where(lane == LEVELS + level, par_s[level], row)
    meta[n] = row
    for kv in range(2):
        arrived(sources[kv], loc_sem.at[kv])
    pl.semaphore_wait(barrier, (MP - 1) + (len(NEAR) - 1) * MP + (NZ - 3))

    for kv, near in HOPS:
        dz, dy = NEAR[near]
        dst = gathered[kv].at[n, own_tok]
        for d in range(1, MP):
            p = peer(d)
            to_any(sources[kv].at[own_class, :, pl.ds(p * HD, HD)], dst, HOP, hop_rs.at[HOPS.index((kv, near))], node(dz, dy), p)
        src = sources[kv].at[own_class, :, own_lanes]
        if near:
            to_node(src, dst, HOP, hop_rs.at[HOPS.index((kv, near))], node(dz, dy))
        else:
            local(src, dst, hop_rs.at[HOPS.index((kv, near))])
    for d in range(1, NY):
        to_node(meta.at[n], meta.at[n], META, meta_rs.at[0], node(0, d))
    for kv in range(2):
        for d in range(1, MP):
            p = peer(d)
            to_mp(sources[kv].at[:, :, pl.ds(p * HD, HD)], kvl.at[kv, :, own_tok], SHARE, a2a_rs.at[kv], p)
        local(sources[kv].at[:, :, own_lanes], kvl.at[kv, :, own_tok], a2a_rs.at[kv])

    def hop_wait(kv, near):
        dz, dy = NEAR[near]
        arrived(gathered[kv].at[node(-dz, -dy)], hop_rs.at[HOPS.index((kv, near))])

    def piece(slot, col):
        return gathered[VALUE if col == 4 else KEY].at[slot]

    def ag_z(col, direction, s):
        sign = 1 if direction == 0 else -1
        src = piece(node(-sign * (s - 1), 0 if col == 4 else col), col)
        to_node(src, src, GATHER, agz_rs.at[AGZ[col, direction, s]], node(sign, 0))

    def ag_z_wait(col, direction, s):
        if col == 4 and s == 1:
            hop_wait(VALUE, 4 + direction)
            return
        sign = 1 if direction == 0 else -1
        dst = piece(node(-sign * s, 0 if col == 4 else col), col)
        arrived(dst, agz_rs.at[AGZ[col, direction, s]])

    def ag_y(t):
        src = piece(node(t, 0), 4)
        for d in (2, 1, 3):
            to_node(src, src, GATHER, agy_rs.at[0], node(0, d))

    def gather_start():
        hop_wait(KEY, 0)
        for direction in range(2):
            ag_z(0, direction, 1)
        hop_wait(VALUE, 0)
        ag_y(0)
        for d in (1, 3, 2):
            hop_wait(KEY, d)
            for direction in range(2):
                ag_z(NY - d, direction, 1)

    def gather_round(s):
        for col in (4, 0, 3, 1, 2):
            for direction in range(2):
                reach = REACH[col][direction]
                if s > reach:
                    continue
                ag_z_wait(col, direction, s)
                if s < reach:
                    ag_z(col, direction, s + 1)
                if col == 4:
                    ag_y((-s if direction == 0 else s) % NZ)

    def gather_end():
        arrived(vg.at[pl.ds(0, (NY - 1) * NZ)], agy_rs.at[0])

    def parent(a, slot):
        return meta_s[slot, 0, LEVELS + a]

    def length(level, slot):
        return meta_s[slot, 0, level]

    def limits(level):
        return [length(a, chains[level][a]) for a in range(level)] + [length(level, n)]

    def fill_context(level, kv, dst):
        first, _ = context(level)
        for a in range(level):
            dst[first + a * SEG:first + (a + 1) * SEG, :] = gathered[kv][chains[level][a]]
        dst[first + level * SEG:first + (level + 1) * SEG, :] = kvl[kv, level]

    def live_rows(level):
        return lax.broadcasted_iota(jnp.int32, (SEG, HD), 0) < length(level, n)

    def probabilities(level):
        first, ctx = context(level)
        fill_context(level, KEY, kc)
        live = live_rows(level)
        for g in range(GROUPS):
            rows = slice(g * SEG, (g + 1) * SEG)
            dos[level, rows, :] = jnp.where(live, dos[level, rows, :], jnp.zeros((), BF16))
        span = slice(first, first + ctx)
        st[span, :] = dot(kc[span, :], qs[level], 1, 1)
        limit = limits(level)
        peak = jnp.full((8, QR), -jnp.inf, F32)
        for r in range(0, ctx, CH):
            b, off = r // SEG, r % SEG
            place = lax.broadcasted_iota(jnp.int32, (CH, QR), 0) + off
            ok = place < limit[b]
            if b == level:
                ok = ok & (place <= (lax.broadcasted_iota(jnp.int32, (CH, QR), 1) & (SEG - 1)))
            s = jnp.where(ok, st[first + r:first + r + CH, :], -jnp.inf)
            st[first + r:first + r + CH, :] = s
            for i in range(0, CH, 8):
                peak = jnp.maximum(peak, s[i:i + 8, :])
        peak = jnp.max(peak, axis=0, keepdims=True)
        total = jnp.zeros((8, QR), F32)
        for r in range(first, first + ctx, CH):
            e = jnp.exp2((st[r:r + CH, :] - peak) * EXP2_SCALE)
            st[r:r + CH, :] = e
            for i in range(0, CH, 8):
                total = total + e[i:i + 8, :]
        inv = 1.0 / jnp.sum(total, axis=0, keepdims=True)
        for r in range(first, first + ctx, CH):
            p = st[r:r + CH, :] * inv
            st[r:r + CH, :] = p
            plow[r:r + CH, :] = p.astype(BF16)
        term[VALUE, span, :] = dot(plow[span, :], dos[level], 1, 0)

    def score_grads(level):
        first, ctx = context(level)
        span = slice(first, first + ctx)
        fill_context(level, VALUE, vc)
        dp[:ctx, :] = dot(vc[span, :], dos[level], 1, 1)
        inner = jnp.zeros((8, QR), F32)
        for r in range(0, ctx, CH):
            prod = st[first + r:first + r + CH, :] * dp[r:r + CH, :]
            for i in range(0, CH, 8):
                inner = inner + prod[i:i + 8, :]
        inner = jnp.sum(inner, axis=0, keepdims=True)
        for r in range(0, ctx, CH):
            g = st[first + r:first + r + CH, :] * (dp[r:r + CH, :] - inner)
            dsl[first + r:first + r + CH, :] = g.astype(BF16)
        term[KEY, span, :] = dot(dsl[span, :], qs[level], 1, 0) * SCALE

    def outputs(level):
        first, ctx = context(level)
        span = slice(first, first + ctx)
        live = live_rows(level)
        out_t = dot(vc[span, :], plow[span, :], 0, 0)
        gq_t = dot(kc[span, :], dsl[span, :], 0, 0) * SCALE
        for g in range(GROUPS):
            cols = slice(g * SEG, (g + 1) * SEG)
            att_v[level, :, cols] = jnp.where(live, jnp.transpose(out_t[:, cols]), 0.0).astype(BF16)
            gq_v[level, :, cols] = jnp.transpose(gq_t[:, cols]).astype(BF16)
        for i, (src, dst) in enumerate(((att_v, att_hbm), (gq_v, gq_hbm))):
            local(src.at[level], dst.at[level], loc_sem.at[4 + i])

    def term_sums(kv):
        for a in range(LEVELS - 1):
            names = list(range(a + 1, LEVELS))
            for bits in range(1 << len(names)):
                slot = kv * SETS + a * 8 + (bits << a)
                for r in range(0, SEG, CH):
                    acc = None
                    for i, level in enumerate(names):
                        if bits >> i & 1:
                            start = context(level)[0] + a * SEG + r
                            x = term[kv, start:start + CH, :]
                            acc = x if acc is None else acc + x
                    if acc is None:
                        acc = jnp.zeros((CH, HD), F32)
                    cbuf[slot, r:r + CH, :] = acc.astype(BF16)

    def own_part(target, col):
        return cbuf[(KEY if col == 4 else VALUE) * SETS + set_s[target]].astype(F32)

    def spread(t):
        for d in (2, 1, 3):
            sy[t, d - 1] = own_part(node(t, d), 4).astype(BF16)
            to_node(sy.at[t, d - 1], ry.at[t, d - 1], SCATTER, rsy_rs.at[t], node(0, d))

    def total_b(t):
        acc = own_part(node(t, 0), 4)
        arrived(ry.at[t], rsy_rs.at[t])
        for d in range(1, NY):
            acc = acc + ry[t, d - 1].astype(F32)
        return acc

    def rs_z(col, direction, t, first):
        src = rz0.at[col, direction] if first else rz.at[col, direction, t]
        to_node(src, rz.at[col, direction, t - 1], SCATTER, rsz_rs.at[RSZ[col, direction, t - 1]],
                node(1 if direction == 0 else -1, 0))

    def rs_z_wait(col, direction, t):
        arrived(rz.at[col, direction, t], rsz_rs.at[RSZ[col, direction, t]])

    def last_hop(kv, near, acc):
        dz, dy = NEAR[near]
        last[kv, near] = acc.astype(BF16)
        dst = got.at[kv, near, m]
        for d in range(1, MP):
            p = peer(d)
            to_any(last.at[kv, near, pl.ds(p * TOK, TOK)], dst, LAST, end_rs.at[ENDS.index((kv, near))], node(dz, dy), p)
        src = last.at[kv, near, own_tok]
        if near:
            to_node(src, dst, LAST, end_rs.at[ENDS.index((kv, near))], node(dz, dy))
        else:
            local(src, dst, end_rs.at[ENDS.index((kv, near))])

    def last_sum(kv):
        nears = [near for k, near in ENDS if k == kv]
        for near in nears:
            arrived(got.at[kv, near], end_rs.at[ENDS.index((kv, near))])
        for head in range(MP):
            acc = sum(got[kv, near, head].astype(F32) for near in nears)
            rows_out[kv, :, head * HD:(head + 1) * HD] = acc.astype(BF16)
        local(rows_out.at[kv], results[kv].at[own_class], loc_sem.at[6])

    def chain(col, step):
        for direction in range(2):
            t = REACH[col][direction] - step
            if t < 0 or (col == 4 and t == 0):
                continue
            if step > 0:
                rs_z_wait(col, direction, t)
            if t == 0:
                continue
            rel = t if direction == 0 else -t
            acc = total_b(rel % NZ) if col == 4 else own_part(node(rel, col), col)
            if step > 0:
                acc = acc + rz[col, direction, t].astype(F32)
            if col == 4 and t == 1:
                last_hop(KEY, 4 + direction, acc)
                continue
            if step == 0:
                rz0[col, direction] = acc.astype(BF16)
            else:
                rz[col, direction, t] = acc.astype(BF16)
            rs_z(col, direction, t, step == 0)

    def ring_step(step):
        for col in COLS:
            chain(col, step)

    def ring_turn():
        for col in COLS:
            chain(col, 4)
            acc = own_part(node(0, col), col) + rz[col, 0, 0].astype(F32) + rz[col, 1, 0].astype(F32)
            if col == 0:
                acc = acc + own_term(VALUE, pl.ds(own_start(own_class), SEG))
            last_hop(VALUE, col, acc)

    def spread_turn():
        last_hop(KEY, 0, total_b(0) + own_term(KEY, pl.ds(own_start(own_class), SEG)))

    def send_back(kv, level):
        dst = results[kv].at[level, :, own_lanes]
        for d in range(1, MP):
            p = peer(d)
            to_mp(gfin.at[kv, level, pl.ds(p * TOK, TOK)], dst, BACK, back_rs.at[kv], p)
        local(gfin.at[kv, level, own_tok], dst, back_rs.at[kv])

    def own_term(kv, level_rows):
        return term[kv, level_rows, :]

    def own_start(level):
        return (level * (level + 3) // 2) * SEG

    def finish_own(kv):
        for i in range(1, LEVELS):
            level = lax.rem(own_class + i, LEVELS)
            gfin[kv, level] = own_term(kv, pl.ds(own_start(level), SEG)).astype(BF16)
            send_back(kv, level)

    gather_start()
    my_row = pl.ds(node(0, 0) - y, NY)
    arrived(meta.at[pl.ds(0, NY - 1)], meta_rs.at[0])
    for d in range(1, NZ):
        to_node(meta.at[my_row], meta.at[my_row], META, meta_rs.at[1], node(d, 0))
    gather_round(1)
    gather_round(2)
    arrived(meta.at[pl.ds(0, NODES - NY)], meta_rs.at[1])
    local(meta, meta_s, loc_sem.at[7])
    pltpu.make_async_copy(meta, meta_s, loc_sem.at[7]).wait()
    chains = []
    for level in range(LEVELS):
        links = [None] * level
        slot = n
        for a in reversed(range(level)):
            slot = parent(a, slot)
            links[a] = slot
        chains.append(links)
    for target in range(NODES):
        a = target % (LEVELS - 1)
        slot = jnp.int32(a * 8)
        for level in range(a + 1, LEVELS):
            slot = slot + (chains[level][a] == target).astype(jnp.int32) * (1 << (level - 1))
        set_s[target] = slot
    gather_round(3)
    arrived(qs, loc_sem.at[2])
    arrived(dos, loc_sem.at[3])
    for kv in range(2):
        arrived(kvl.at[kv], a2a_rs.at[kv])
    gather_round(4)
    probabilities(3)
    probabilities(2)
    probabilities(1)
    term_sums(VALUE)
    ring_step(0)
    gather_end()
    score_grads(3)
    score_grads(2)
    score_grads(1)
    term_sums(KEY)
    spread(4)
    spread(5)
    ring_step(1)
    spread(3)
    spread(6)
    chain(4, 0)
    spread(2)
    spread(7)
    probabilities(0)
    ring_step(2)
    chain(4, 1)
    spread(1)
    spread(0)
    finish_own(VALUE)
    score_grads(0)
    ring_step(3)
    chain(4, 2)
    finish_own(KEY)
    outputs(3)
    ring_turn()
    chain(4, 3)
    spread_turn()
    outputs(2)
    outputs(1)
    outputs(0)
    last_sum(VALUE)
    last_sum(KEY)
    for kv in (VALUE, KEY):
        arrived(results[kv].at[pl.ds(0, LEVELS - 1)], back_rs.at[kv])
    arrived(att_v, loc_sem.at[4])
    arrived(gq_v, loc_sem.at[5])
    arrived(rows_out, loc_sem.at[6])
    units = {HOP: len(HOPS) * MP - 2, SHARE: 2 * (MP - 1) * LEVELS, GATHER: 57 * MP, SCATTER: 57 * MP,
             LAST: len(HOPS) * MP - 2, BACK: 2 * (MP - 1) * (LEVELS - 1)}
    for kind, count in units.items():
        arrived(sent.at[pl.ds(0, count)], send_sem.at[kind])
    arrived(meta.at[pl.ds(0, NODES - 1)], send_sem.at[META])


def store(pieces, *refs):
    src, dst, buf, (load_sem, store_sem) = refs[:4], refs[4:8], refs[8:12], refs[12:]

    def part(arrays, piece):
        i, level = piece
        return arrays[i] if level is None else arrays[i].at[level]

    loads = [pltpu.make_async_copy(part(src, p), part(buf, p), load_sem.at[k]) for k, p in enumerate(pieces)]
    stores = [pltpu.make_async_copy(part(buf, p), part(dst, p), store_sem.at[k]) for k, p in enumerate(pieces)]
    for c in loads:
        c.start()
    for a, b in zip(loads, stores):
        a.wait()
        b.start()
    for c in stores:
        c.wait()


def per_device(queries, keys, values, grad_out, lengths, parents):
    hbm = pl.BlockSpec(memory_space=pltpu.HBM)
    smem = pl.BlockSpec(memory_space=pltpu.SMEM)
    dma = pltpu.SemaphoreType.DMA
    vm = pltpu.VMEM
    ctx = LEVELS * SEG
    block = (SEG, HD)
    results = pl.pallas_call(
        kernel,
        out_shape=tuple(jax.ShapeDtypeStruct(x.shape, BF16) for x in (queries, queries, keys, keys)),
        in_specs=[hbm, hbm, hbm, hbm, smem, smem],
        out_specs=(hbm,) * 4,
        scratch_shapes=[
            vm((LEVELS, TOK, MP * HD), BF16), vm((LEVELS, TOK, MP * HD), BF16),
            vm((LEVELS, QR, HD), BF16), vm((LEVELS, QR, HD), BF16),
            vm((2, LEVELS, SEG, HD), BF16), vm((NODES, SEG, HD), BF16), vm((NODES, SEG, HD), BF16),
            vm((NODES, 1, 128), jnp.int32), pltpu.SMEM((NODES, 1, 128), jnp.int32), pltpu.SMEM((NODES,), jnp.int32),
            vm((CTX_ROWS, HD), BF16), vm((CTX_ROWS, HD), BF16),
            vm((CTX_ROWS, QR), F32), vm((ctx, QR), F32), vm((CTX_ROWS, QR), BF16), vm((CTX_ROWS, QR), BF16),
            vm((LEVELS, SEG, QR), BF16), vm((LEVELS, SEG, QR), BF16),
            vm((2, CTX_ROWS, HD), F32), vm((2 * SETS, SEG, HD), BF16), vm((2, LEVELS, SEG, HD), BF16),
            vm((5, 2, 4) + block, BF16), vm((5, 2) + block, BF16),
            vm((NZ, NY - 1) + block, BF16), vm((NZ, NY - 1) + block, BF16),
            vm((2, len(NEAR)) + block, BF16), vm((2, len(NEAR), MP, TOK, HD), BF16), vm((2, TOK, MP * HD), BF16),
            vm((57 * MP, TOK, HD), BF16),
            dma((8,)), dma((7,)), dma((2,)), dma((2,)), dma((len(HOPS),)), dma((len(AGZ),)), dma((1,)),
            dma((len(RSZ),)), dma((NZ,)), dma((len(HOPS),)), dma((2,)),
        ],
        compiler_params=pltpu.CompilerParams(collective_id=0, has_side_effects=True, vmem_limit_bytes=60 << 20),
        name="tree_attention",
    )(queries, keys, values, grad_out, lengths.reshape(LEVELS), parents.reshape(LEVELS - 1))
    pieces = [(i, level) for i in range(2) for level in range(LEVELS)] + [(2, None), (3, None)]
    return tuple(pl.pallas_call(
        functools.partial(store, pieces),
        out_shape=tuple(jax.ShapeDtypeStruct(x.shape, BF16) for x in results),
        in_specs=[hbm] * 4,
        out_specs=(hbm,) * 4,
        scratch_shapes=[vm(x.shape, BF16) for x in results] + [dma((len(pieces),)), dma((len(pieces),))],
        name="store",
    )(*results))


def solution(mesh):
    placed = (
        P(None, "node", "mp"),
        P(None, ("node", "mp"), None),
        P(None, ("node", "mp"), None),
        P(None, "node", "mp"),
        P(None, "node"),
        P(None, "node"),
    )
    return jax.shard_map(
        per_device,
        mesh=mesh,
        in_specs=placed,
        out_specs=(
            P(None, "node", "mp"),
            P(None, "node", "mp"),
            P(None, ("node", "mp"), None),
            P(None, ("node", "mp"), None),
        ),
        check_vma=False,
    )
```

```python
import functools
import math

import jax
import jax.numpy as jnp
from jax import lax
from jax.experimental import pallas as pl
from jax.experimental.pallas import tpu as pltpu
from jax.sharding import PartitionSpec as P

HD = 128
SEG = 128
NZ, NY = 8, 4
NODES = NZ * NY
MP = 8
LEVELS = 4
GROUPS = 5
QR = GROUPS * SEG
TOK = SEG // MP
CTX_ROWS = SEG * LEVELS * (LEVELS + 1) // 2
SETS = 24
F32 = jnp.float32
BF16 = jnp.bfloat16
MESH = pl.DeviceIdType.MESH
SCALE = 1.0 / math.sqrt(HD)
EXP2_SCALE = SCALE * math.log2(math.e)
CH = 32
KEY, VALUE = 0, 1
HOP, META, SHARE, GATHER, SCATTER, LAST, BACK = range(7)
REACH = [(4, 3), (3, 4), (4, 3), (3, 4), (4, 3)]
COLS = (2, 1, 3, 0)
STEPS = [(c, i, s) for c in range(5) for i in range(2) for s in range(REACH[c][i])]
AGZ = {(c, i, s + 1): k for k, (c, i, s) in enumerate(x for x in STEPS if x[0] < 4 or x[2])}
RSZ = {x: k for k, x in enumerate(x for x in STEPS if x[0] < 4 or x[2])}
NEAR = [(0, 0), (0, 1), (0, 2), (0, 3), (1, 0), (-1, 0)]
ENDS = [(VALUE, 0), (VALUE, 1), (VALUE, 2), (VALUE, 3), (KEY, 0), (KEY, 4), (KEY, 5)]
HOPS = [(KEY, 0), (VALUE, 0), (VALUE, 4), (VALUE, 5), (KEY, 1), (KEY, 3), (KEY, 2)]


def dot(a, b, ca, cb):
    return lax.dot_general(a, b, (((ca,), (cb,)), ((), ())), preferred_element_type=F32)


def context(level):
    first = SEG * level * (level + 1) // 2
    return first, (level + 1) * SEG


def kernel(q_hbm, k_hbm, v_hbm, do_hbm, len_s, par_s,
           att_hbm, gq_hbm, gk_o, gv_o,
           ksrc, vsrc, qs, dos, kvl, kg, vg, meta, meta_s, set_s,
           kc, vc, st, dp, plow, dsl, att_v, gq_v, term, cbuf, gfin,
           rz, rz0, ry, sy, last, got, rows_out,
           sent, loc_sem, send_sem, meta_rs, a2a_rs, hop_rs, agz_rs, agy_rs, rsz_rs, rsy_rs, end_rs, back_rs):
    n = lax.axis_index("node")
    m = lax.axis_index("mp")
    z = n >> 2
    y = n & (NY - 1)
    own_class = lax.rem(n, LEVELS - 1)
    sources = (ksrc, vsrc)
    results = (gk_o, gv_o)
    gathered = (kg, vg)

    def node(dz, dy):
        up = ((z + dz) & (NZ - 1)) << 2 if dz % NZ else z << 2
        return up | ((y + dy) & (NY - 1) if dy % NY else y)

    def peer(d):
        return (m + d) & (MP - 1)

    def remote(src, dst, ss, rs, to):
        pltpu.make_async_remote_copy(src_ref=src, dst_ref=dst, send_sem=send_sem.at[ss], recv_sem=rs,
                                     device_id=to, device_id_type=MESH).start()

    def to_node(src, dst, ss, rs, target):
        remote(src, dst, ss, rs, {"node": target})

    def to_mp(src, dst, ss, rs, target):
        remote(src, dst, ss, rs, {"mp": target})

    def to_any(src, dst, ss, rs, target, p):
        remote(src, dst, ss, rs, {"node": target, "mp": p})

    def arrived(ref, sem):
        pltpu.make_async_copy(ref, ref, sem).wait()

    def local(src, dst, sem):
        pltpu.make_async_copy(src, dst, sem).start()

    barrier = pltpu.get_barrier_semaphore()
    for d in (4, 3, 5, 2, 6):
        pl.semaphore_signal(barrier, inc=1, device_id={"node": node(d, 0)}, device_id_type=MESH)
    for near in (2, 1, 3, 4, 5, 0):
        for d in (4, 3, 5, 2, 6, 1, 7, 0):
            if near or d:
                pl.semaphore_signal(barrier, inc=1, device_id={"node": node(*NEAR[near]), "mp": peer(d)}, device_id_type=MESH)

    own_tok = pl.ds(m * TOK, TOK)
    own_lanes = pl.ds(m * HD, HD)
    for kv, src in enumerate((k_hbm, v_hbm)):
        local(src, sources[kv], loc_sem.at[kv])
    for g in range(GROUPS):
        lanes = pl.ds(g * HD, HD)
        for i, (src, dst) in enumerate(((q_hbm, qs), (do_hbm, dos))):
            local(src.at[:, :, lanes], dst.at[:, pl.ds(g * SEG, SEG), :], loc_sem.at[2 + i])

    lane = lax.broadcasted_iota(jnp.int32, (1, 128), 1)
    row = jnp.zeros((1, 128), jnp.int32)
    for level in range(LEVELS):
        row = jnp.where(lane == level, len_s[level], row)
    for level in range(LEVELS - 1):
        row = jnp.where(lane == LEVELS + level, par_s[level], row)
    meta[n] = row
    for kv in range(2):
        arrived(sources[kv], loc_sem.at[kv])
    pl.semaphore_wait(barrier, (MP - 1) + (len(NEAR) - 1) * MP + (NZ - 3))

    for kv, near in HOPS:
        dz, dy = NEAR[near]
        dst = gathered[kv].at[n, own_tok]
        for d in range(1, MP):
            p = peer(d)
            to_any(sources[kv].at[own_class, :, pl.ds(p * HD, HD)], dst, HOP, hop_rs.at[HOPS.index((kv, near))], node(dz, dy), p)
        src = sources[kv].at[own_class, :, own_lanes]
        if near:
            to_node(src, dst, HOP, hop_rs.at[HOPS.index((kv, near))], node(dz, dy))
        else:
            local(src, dst, hop_rs.at[HOPS.index((kv, near))])
    for d in range(1, NY):
        to_node(meta.at[n], meta.at[n], META, meta_rs.at[0], node(0, d))
    def hop_wait(kv, near):
        dz, dy = NEAR[near]
        arrived(gathered[kv].at[node(-dz, -dy)], hop_rs.at[HOPS.index((kv, near))])

    def piece(slot, col):
        return gathered[VALUE if col == 4 else KEY].at[slot]

    def ag_z(col, direction, s):
        sign = 1 if direction == 0 else -1
        src = piece(node(-sign * (s - 1), 0 if col == 4 else col), col)
        to_node(src, src, GATHER, agz_rs.at[AGZ[col, direction, s]], node(sign, 0))

    def ag_z_wait(col, direction, s):
        if col == 4 and s == 1:
            hop_wait(VALUE, 4 + direction)
            return
        sign = 1 if direction == 0 else -1
        dst = piece(node(-sign * s, 0 if col == 4 else col), col)
        arrived(dst, agz_rs.at[AGZ[col, direction, s]])

    def ag_y(t):
        src = piece(node(t, 0), 4)
        for d in (2, 1, 3):
            to_node(src, src, GATHER, agy_rs.at[0], node(0, d))

    def gather_start():
        hop_wait(KEY, 0)
        for direction in range(2):
            ag_z(0, direction, 1)
        hop_wait(VALUE, 0)
        ag_y(0)
        for d in (1, 3, 2):
            hop_wait(KEY, d)
            for direction in range(2):
                ag_z(NY - d, direction, 1)

    def gather_round(s):
        for col in (4, 0, 3, 1, 2):
            for direction in range(2):
                reach = REACH[col][direction]
                if s > reach:
                    continue
                ag_z_wait(col, direction, s)
                if s < reach:
                    ag_z(col, direction, s + 1)
                if col == 4:
                    ag_y((-s if direction == 0 else s) % NZ)

    def gather_end():
        arrived(vg.at[pl.ds(0, (NY - 1) * NZ)], agy_rs.at[0])

    def parent(a, slot):
        return meta_s[slot, 0, LEVELS + a]

    def length(level, slot):
        return meta_s[slot, 0, level]

    def limits(level):
        return [length(a, chains[level][a]) for a in range(level)] + [length(level, n)]

    def fill_context(level, kv, dst):
        first, _ = context(level)
        for a in range(level):
            dst[first + a * SEG:first + (a + 1) * SEG, :] = gathered[kv][chains[level][a]]
        dst[first + level * SEG:first + (level + 1) * SEG, :] = kvl[kv, level]

    def live_rows(level):
        return lax.broadcasted_iota(jnp.int32, (SEG, HD), 0) < length(level, n)

    def probabilities(level):
        first, ctx = context(level)
        fill_context(level, KEY, kc)
        live = live_rows(level)
        for g in range(GROUPS):
            rows = slice(g * SEG, (g + 1) * SEG)
            dos[level, rows, :] = jnp.where(live, dos[level, rows, :], jnp.zeros((), BF16))
        span = slice(first, first + ctx)
        st[span, :] = dot(kc[span, :], qs[level], 1, 1)
        limit = limits(level)
        peak = jnp.full((8, QR), -jnp.inf, F32)
        for r in range(0, ctx, CH):
            b, off = r // SEG, r % SEG
            place = lax.broadcasted_iota(jnp.int32, (CH, QR), 0) + off
            ok = place < limit[b]
            if b == level:
                ok = ok & (place <= (lax.broadcasted_iota(jnp.int32, (CH, QR), 1) & (SEG - 1)))
            s = jnp.where(ok, st[first + r:first + r + CH, :], -jnp.inf)
            st[first + r:first + r + CH, :] = s
            for i in range(0, CH, 8):
                peak = jnp.maximum(peak, s[i:i + 8, :])
        peak = jnp.max(peak, axis=0, keepdims=True)
        total = jnp.zeros((8, QR), F32)
        for r in range(first, first + ctx, CH):
            e = jnp.exp2((st[r:r + CH, :] - peak) * EXP2_SCALE)
            st[r:r + CH, :] = e
            for i in range(0, CH, 8):
                total = total + e[i:i + 8, :]
        inv = 1.0 / jnp.sum(total, axis=0, keepdims=True)
        for r in range(first, first + ctx, CH):
            p = st[r:r + CH, :] * inv
            st[r:r + CH, :] = p
            plow[r:r + CH, :] = p.astype(BF16)
        term[VALUE, span, :] = dot(plow[span, :], dos[level], 1, 0)

    def score_grads(level):
        first, ctx = context(level)
        span = slice(first, first + ctx)
        fill_context(level, VALUE, vc)
        dp[:ctx, :] = dot(vc[span, :], dos[level], 1, 1)
        inner = jnp.zeros((8, QR), F32)
        for r in range(0, ctx, CH):
            prod = st[first + r:first + r + CH, :] * dp[r:r + CH, :]
            for i in range(0, CH, 8):
                inner = inner + prod[i:i + 8, :]
        inner = jnp.sum(inner, axis=0, keepdims=True)
        for r in range(0, ctx, CH):
            g = st[first + r:first + r + CH, :] * (dp[r:r + CH, :] - inner)
            dsl[first + r:first + r + CH, :] = g.astype(BF16)
        term[KEY, span, :] = dot(dsl[span, :], qs[level], 1, 0) * SCALE

    def outputs(level):
        first, ctx = context(level)
        span = slice(first, first + ctx)
        live = live_rows(level)
        out_t = dot(vc[span, :], plow[span, :], 0, 0)
        gq_t = dot(kc[span, :], dsl[span, :], 0, 0) * SCALE
        for g in range(GROUPS):
            cols = slice(g * SEG, (g + 1) * SEG)
            att_v[level, :, cols] = jnp.where(live, jnp.transpose(out_t[:, cols]), 0.0).astype(BF16)
            gq_v[level, :, cols] = jnp.transpose(gq_t[:, cols]).astype(BF16)
        for i, (src, dst) in enumerate(((att_v, att_hbm), (gq_v, gq_hbm))):
            local(src.at[level], dst.at[level], loc_sem.at[4 + i])

    def term_sums(kv):
        for a in range(LEVELS - 1):
            names = list(range(a + 1, LEVELS))
            for bits in range(1 << len(names)):
                slot = kv * SETS + a * 8 + (bits << a)
                for r in range(0, SEG, CH):
                    acc = None
                    for i, level in enumerate(names):
                        if bits >> i & 1:
                            start = context(level)[0] + a * SEG + r
                            x = term[kv, start:start + CH, :]
                            acc = x if acc is None else acc + x
                    if acc is None:
                        acc = jnp.zeros((CH, HD), F32)
                    cbuf[slot, r:r + CH, :] = acc.astype(BF16)

    def own_part(target, col):
        return cbuf[(KEY if col == 4 else VALUE) * SETS + set_s[target]].astype(F32)

    def spread(t):
        for d in (2, 1, 3):
            sy[t, d - 1] = own_part(node(t, d), 4).astype(BF16)
            to_node(sy.at[t, d - 1], ry.at[t, d - 1], SCATTER, rsy_rs.at[t], node(0, d))

    def total_b(t):
        acc = own_part(node(t, 0), 4)
        arrived(ry.at[t], rsy_rs.at[t])
        for d in range(1, NY):
            acc = acc + ry[t, d - 1].astype(F32)
        return acc

    def rs_z(col, direction, t, first):
        src = rz0.at[col, direction] if first else rz.at[col, direction, t]
        to_node(src, rz.at[col, direction, t - 1], SCATTER, rsz_rs.at[RSZ[col, direction, t - 1]],
                node(1 if direction == 0 else -1, 0))

    def rs_z_wait(col, direction, t):
        arrived(rz.at[col, direction, t], rsz_rs.at[RSZ[col, direction, t]])

    def last_hop(kv, near, acc):
        dz, dy = NEAR[near]
        last[kv, near] = acc.astype(BF16)
        dst = got.at[kv, near, m]
        for d in range(1, MP):
            p = peer(d)
            to_any(last.at[kv, near, pl.ds(p * TOK, TOK)], dst, LAST, end_rs.at[ENDS.index((kv, near))], node(dz, dy), p)
        src = last.at[kv, near, own_tok]
        if near:
            to_node(src, dst, LAST, end_rs.at[ENDS.index((kv, near))], node(dz, dy))
        else:
            local(src, dst, end_rs.at[ENDS.index((kv, near))])

    def last_sum(kv):
        nears = [near for k, near in ENDS if k == kv]
        for near in nears:
            arrived(got.at[kv, near], end_rs.at[ENDS.index((kv, near))])
        for head in range(MP):
            acc = sum(got[kv, near, head].astype(F32) for near in nears)
            rows_out[kv, :, head * HD:(head + 1) * HD] = acc.astype(BF16)
        local(rows_out.at[kv], results[kv].at[own_class], loc_sem.at[6])

    def chain(col, step):
        for direction in range(2):
            t = REACH[col][direction] - step
            if t < 0 or (col == 4 and t == 0):
                continue
            if step > 0:
                rs_z_wait(col, direction, t)
            if t == 0:
                continue
            rel = t if direction == 0 else -t
            acc = total_b(rel % NZ) if col == 4 else own_part(node(rel, col), col)
            if step > 0:
                acc = acc + rz[col, direction, t].astype(F32)
            if col == 4 and t == 1:
                last_hop(KEY, 4 + direction, acc)
                continue
            if step == 0:
                rz0[col, direction] = acc.astype(BF16)
            else:
                rz[col, direction, t] = acc.astype(BF16)
            rs_z(col, direction, t, step == 0)

    def ring_step(step):
        for col in COLS:
            chain(col, step)

    def ring_turn():
        for col in COLS:
            chain(col, 4)
            acc = own_part(node(0, col), col) + rz[col, 0, 0].astype(F32) + rz[col, 1, 0].astype(F32)
            if col == 0:
                acc = acc + own_term(VALUE, pl.ds(own_start(own_class), SEG))
            last_hop(VALUE, col, acc)

    def spread_turn():
        last_hop(KEY, 0, total_b(0) + own_term(KEY, pl.ds(own_start(own_class), SEG)))

    def send_back(kv, level):
        dst = results[kv].at[level, :, own_lanes]
        for d in range(1, MP):
            p = peer(d)
            to_mp(gfin.at[kv, level, pl.ds(p * TOK, TOK)], dst, BACK, back_rs.at[kv], p)
        local(gfin.at[kv, level, own_tok], dst, back_rs.at[kv])

    def own_term(kv, level_rows):
        return term[kv, level_rows, :]

    def own_start(level):
        return (level * (level + 3) // 2) * SEG

    def finish_own(kv):
        for i in range(1, LEVELS):
            level = lax.rem(own_class + i, LEVELS)
            gfin[kv, level] = own_term(kv, pl.ds(own_start(level), SEG)).astype(BF16)
            send_back(kv, level)

    gather_start()
    for kv in range(2):
        for d in range(1, MP):
            p = peer(d)
            to_mp(sources[kv].at[:, :, pl.ds(p * HD, HD)], kvl.at[kv, :, own_tok], SHARE, a2a_rs.at[kv], p)
        local(sources[kv].at[:, :, own_lanes], kvl.at[kv, :, own_tok], a2a_rs.at[kv])
    my_row = pl.ds(node(0, 0) - y, NY)
    arrived(meta.at[pl.ds(0, NY - 1)], meta_rs.at[0])
    for d in range(1, NZ):
        to_node(meta.at[my_row], meta.at[my_row], META, meta_rs.at[1], node(d, 0))
    gather_round(1)
    gather_round(2)
    arrived(meta.at[pl.ds(0, NODES - NY)], meta_rs.at[1])
    local(meta, meta_s, loc_sem.at[7])
    pltpu.make_async_copy(meta, meta_s, loc_sem.at[7]).wait()
    chains = []
    for level in range(LEVELS):
        links = [None] * level
        slot = n
        for a in reversed(range(level)):
            slot = parent(a, slot)
            links[a] = slot
        chains.append(links)
    for target in range(NODES):
        a = target % (LEVELS - 1)
        slot = jnp.int32(a * 8)
        for level in range(a + 1, LEVELS):
            slot = slot + (chains[level][a] == target).astype(jnp.int32) * (1 << (level - 1))
        set_s[target] = slot
    gather_round(3)
    arrived(qs, loc_sem.at[2])
    arrived(dos, loc_sem.at[3])
    for kv in range(2):
        arrived(kvl.at[kv], a2a_rs.at[kv])
    gather_round(4)
    probabilities(3)
    probabilities(2)
    probabilities(1)
    term_sums(VALUE)
    ring_step(0)
    gather_end()
    score_grads(3)
    score_grads(2)
    score_grads(1)
    term_sums(KEY)
    spread(4)
    spread(5)
    ring_step(1)
    spread(3)
    spread(6)
    chain(4, 0)
    spread(2)
    spread(7)
    probabilities(0)
    ring_step(2)
    chain(4, 1)
    spread(1)
    spread(0)
    finish_own(VALUE)
    score_grads(0)
    ring_step(3)
    chain(4, 2)
    finish_own(KEY)
    outputs(3)
    ring_turn()
    chain(4, 3)
    spread_turn()
    outputs(2)
    outputs(1)
    outputs(0)
    last_sum(VALUE)
    last_sum(KEY)
    for kv in (VALUE, KEY):
        arrived(results[kv].at[pl.ds(0, LEVELS - 1)], back_rs.at[kv])
    arrived(att_v, loc_sem.at[4])
    arrived(gq_v, loc_sem.at[5])
    arrived(rows_out, loc_sem.at[6])
    units = {HOP: len(HOPS) * MP - 2, SHARE: 2 * (MP - 1) * LEVELS, GATHER: 57 * MP, SCATTER: 57 * MP,
             LAST: len(HOPS) * MP - 2, BACK: 2 * (MP - 1) * (LEVELS - 1)}
    for kind, count in units.items():
        arrived(sent.at[pl.ds(0, count)], send_sem.at[kind])
    arrived(meta.at[pl.ds(0, NODES - 1)], send_sem.at[META])


def store(pieces, *refs):
    src, dst, buf, (load_sem, store_sem) = refs[:4], refs[4:8], refs[8:12], refs[12:]

    def part(arrays, piece):
        i, level = piece
        return arrays[i] if level is None else arrays[i].at[level]

    loads = [pltpu.make_async_copy(part(src, p), part(buf, p), load_sem.at[k]) for k, p in enumerate(pieces)]
    stores = [pltpu.make_async_copy(part(buf, p), part(dst, p), store_sem.at[k]) for k, p in enumerate(pieces)]
    for c in loads:
        c.start()
    for a, b in zip(loads, stores):
        a.wait()
        b.start()
    for c in stores:
        c.wait()


def per_device(queries, keys, values, grad_out, lengths, parents):
    hbm = pl.BlockSpec(memory_space=pltpu.HBM)
    smem = pl.BlockSpec(memory_space=pltpu.SMEM)
    dma = pltpu.SemaphoreType.DMA
    vm = pltpu.VMEM
    ctx = LEVELS * SEG
    block = (SEG, HD)
    results = pl.pallas_call(
        kernel,
        out_shape=tuple(jax.ShapeDtypeStruct(x.shape, BF16) for x in (queries, queries, keys, keys)),
        in_specs=[hbm, hbm, hbm, hbm, smem, smem],
        out_specs=(hbm,) * 4,
        scratch_shapes=[
            vm((LEVELS, TOK, MP * HD), BF16), vm((LEVELS, TOK, MP * HD), BF16),
            vm((LEVELS, QR, HD), BF16), vm((LEVELS, QR, HD), BF16),
            vm((2, LEVELS, SEG, HD), BF16), vm((NODES, SEG, HD), BF16), vm((NODES, SEG, HD), BF16),
            vm((NODES, 1, 128), jnp.int32), pltpu.SMEM((NODES, 1, 128), jnp.int32), pltpu.SMEM((NODES,), jnp.int32),
            vm((CTX_ROWS, HD), BF16), vm((CTX_ROWS, HD), BF16),
            vm((CTX_ROWS, QR), F32), vm((ctx, QR), F32), vm((CTX_ROWS, QR), BF16), vm((CTX_ROWS, QR), BF16),
            vm((LEVELS, SEG, QR), BF16), vm((LEVELS, SEG, QR), BF16),
            vm((2, CTX_ROWS, HD), F32), vm((2 * SETS, SEG, HD), BF16), vm((2, LEVELS, SEG, HD), BF16),
            vm((5, 2, 4) + block, BF16), vm((5, 2) + block, BF16),
            vm((NZ, NY - 1) + block, BF16), vm((NZ, NY - 1) + block, BF16),
            vm((2, len(NEAR)) + block, BF16), vm((2, len(NEAR), MP, TOK, HD), BF16), vm((2, TOK, MP * HD), BF16),
            vm((57 * MP, TOK, HD), BF16),
            dma((8,)), dma((7,)), dma((2,)), dma((2,)), dma((len(HOPS),)), dma((len(AGZ),)), dma((1,)),
            dma((len(RSZ),)), dma((NZ,)), dma((len(HOPS),)), dma((2,)),
        ],
        compiler_params=pltpu.CompilerParams(collective_id=0, has_side_effects=True, vmem_limit_bytes=60 << 20),
        name="tree_attention",
    )(queries, keys, values, grad_out, lengths.reshape(LEVELS), parents.reshape(LEVELS - 1))
    pieces = [(i, level) for i in range(2) for level in range(LEVELS)] + [(2, None), (3, None)]
    return tuple(pl.pallas_call(
        functools.partial(store, pieces),
        out_shape=tuple(jax.ShapeDtypeStruct(x.shape, BF16) for x in results),
        in_specs=[hbm] * 4,
        out_specs=(hbm,) * 4,
        scratch_shapes=[vm(x.shape, BF16) for x in results] + [dma((len(pieces),)), dma((len(pieces),))],
        name="store",
    )(*results))


def solution(mesh):
    placed = (
        P(None, "node", "mp"),
        P(None, ("node", "mp"), None),
        P(None, ("node", "mp"), None),
        P(None, "node", "mp"),
        P(None, "node"),
        P(None, "node"),
    )
    return jax.shard_map(
        per_device,
        mesh=mesh,
        in_specs=placed,
        out_specs=(
            P(None, "node", "mp"),
            P(None, "node", "mp"),
            P(None, ("node", "mp"), None),
            P(None, ("node", "mp"), None),
        ),
        check_vma=False,
    )
```
